32 devices in a mesh: tile: 2 (over y), strip: 4 (over x, core), focus: 4 (over z).
Axes of the slice: x: 2, y: 2, z: 4, core: 2. Of those that a mesh axis runs over, the one named last changes fastest.
Arguments:
- phi: float32 [512, 2048], P(('tile', 'strip')), parts along dimension 0, may hold values from -6 to 6
- target: int32 [512, 2048], P(('tile', 'strip')), parts along dimension 0, may hold values 0 or 1
- defocus_ids: int32 [8], P(('tile', 'focus')), parts along dimension 0, may hold values from 0 to 30
- kernels: float32 [2, 4, 48, 512], replicated, may hold values from -16 to 16
- psi: float32 [48, 512], replicated, may hold values from -3.140625 to 3.140625
- row_freqs: int32 [48], replicated, may hold values from -96 to 95, as said below
- col_freqs: int32 [512], replicated, may hold values from -1024 to 1023, as said below
Outputs:
- phi_next: float32 [512, 2048], P(('tile', 'strip')), parts along dimension 0
The draws below stay inside these ranges and needn't reach their ends.
There are 2 independent parts, one for each index of `tile`. The reference program is written for one: setup_inputs(seed, part) draws one part's arguments, and reference() takes and returns one part's arrays. A program takes and returns all parts, laid end to end along the dimension named above; an argument that names none is the same for every part. Nothing has to cross between parts.
Inputs may be any that keep to these rules, and one draw needn't show every extreme that they name: `row_freqs`: distinct whole frequencies; the lowest and highest of the range are always among them. `col_freqs`: distinct whole frequencies; the lowest and highest of the range are always among them.
All inputs are finite; a program needn't handle non-finite values. No bound on the sum of `target` on one device may be relied on, other than what follows from the above.
Results may differ from the reference program's by a relative error of at most 0.02.
Values may be sent and summed in bfloat16 or wider, within the bound.
A program may use at most 64 MiB of HBM per device.

```python
import jax
import jax.numpy as jnp
from jax import lax

ROWS = 64
MARGIN = 64
COLS = 2048
FR = 48
FC = 512
KERN = 4
LEVELS = 31
SWEEPS = 2
WIN = 192
STRIPS = 4
PLANES = 4


def pick_freqs(key, period, number):
    inner = jax.random.permutation(key, period - 2)[:number - 2] + 1
    picked = jnp.concatenate([jnp.array([0, period - 1], jnp.int32), inner.astype(jnp.int32)])
    return (picked - period // 2).astype(jnp.int32)


def draw_row_freqs(key, part):
    return pick_freqs(jax.random.fold_in(key, 11), WIN, FR)


def draw_col_freqs(key, part):
    return pick_freqs(jax.random.fold_in(key, 23), COLS, FC)


def touch_ends(values, own_key, smallest, high):
    longest = values.shape.index(max(values.shape))
    spots = []
    for shift in (0, 1):
        where = [jax.random.randint(jax.random.fold_in(own_key, axis), (), 0, length) for axis, length in enumerate(values.shape)]
        where[longest] = (where[longest] + shift) % values.shape[longest]
        spots.append(tuple(where))
    return values.at[spots[0]].set(smallest).at[spots[1]].set(high)


def shard_levels(stream_key, shape, split, least, largest):
    loudness, own = 1.0, jax.random.fold_in(stream_key, 6)
    for dim, blocks in split:
        steps = jnp.exp(jax.random.uniform(jax.random.fold_in(own, dim), (blocks,), jnp.float32, least / len(split), largest / len(split)))
        loudness = loudness * jnp.repeat(steps, shape[dim] // blocks).reshape([-1 if axis == dim else 1 for axis in range(len(shape))])
    return loudness


def normal_values(own_key, extent, deviation, bound, pieces=(), kind=jnp.bfloat16):
    level = shard_levels(own_key, extent, pieces, -0.22, 0.18) if pieces else 1.0
    values = jax.random.normal(own_key, extent, jnp.float32) * deviation * level
    return jnp.minimum(jnp.maximum(values, -bound), bound).astype(kind)


def setup_inputs(seed: int = 0, part: int = 0) -> dict:
    splits = jax.random.split(jax.random.key(seed), 8)
    part_keys = jax.random.split(jax.random.fold_in(splits[7], part), 8)
    return {
        "phi": normal_values(part_keys[0], (STRIPS * ROWS, COLS), 1.0, 6.0, ((0, 4),), jnp.float32),
        "target": touch_ends((jax.random.randint(part_keys[1], (STRIPS * ROWS, COLS), 0, 2) < 1).astype(jnp.int32), jax.random.fold_in(part_keys[1], 1), 0, 1),
        "defocus_ids": touch_ends(jax.random.randint(part_keys[2], (PLANES,), 0, LEVELS), jax.random.fold_in(part_keys[2], 1), 0, LEVELS - 1).astype(jnp.int32),
        "kernels": normal_values(splits[3], (2, KERN, FR, FC), 3.0, 16.0, (), jnp.float32),
        "psi": jnp.clip(jax.random.uniform(splits[4], (FR, FC), jnp.float32, -3.140625, 3.140625), -3.140625, 3.140625),
        "row_freqs": draw_row_freqs(jax.random.fold_in(splits[7], 71), part),
        "col_freqs": draw_col_freqs(jax.random.fold_in(splits[7], 71), part),
    }


slope_resist = 4.0
level_resist = 0.5
step_size = 1.0
flow_rate = 0.2

def tables(freq_list, period, length):
    positions = jnp.arange(length, dtype=jnp.int32)
    phase_int = jnp.mod(freq_list[:, None] * positions[None, :], period)
    angles = phase_int.astype(jnp.float32) * (2.0 * jnp.pi / period)
    return (jnp.cos(angles).astype(jnp.bfloat16), jnp.sin(angles).astype(jnp.bfloat16))

def product(lhs_mat, rhs_mat):
    return jnp.dot(lhs_mat, rhs_mat, preferred_element_type=jnp.float32)

def product_t(lhs_mat, rhs_mat):
    return lax.dot_general(lhs_mat, rhs_mat, (((1,), (1,)), ((), ())), preferred_element_type=jnp.float32)

def exact_t(lhs_mat, rhs_mat):
    return lax.dot_general(lhs_mat.astype(jnp.float32), rhs_mat, (((0,), (0,)), ((), ())), precision=lax.Precision.HIGHEST, preferred_element_type=jnp.float32)

def batch(form, lhs_mat, rhs_mat):
    return jnp.einsum(form, lhs_mat.astype(jnp.float32), rhs_mat.astype(jnp.float32), precision=lax.Precision.HIGHEST)

def spectral_rows(cos_part, sin_part, y_re, y_im):
    z_re = exact_t(cos_part, y_re) - exact_t(sin_part, y_im)
    z_im = exact_t(cos_part, y_im) + exact_t(sin_part, y_re)
    return (z_re.astype(jnp.bfloat16), z_im.astype(jnp.bfloat16))

def curvature_step(padded):
    center = padded[1:-1, 1:-1]
    upper_row = padded[2:, 1:-1]
    lower_row = padded[:-2, 1:-1]
    right_col = padded[1:-1, 2:]
    left_col = padded[1:-1, :-2]
    diagonal = padded[2:, 2:] - padded[2:, :-2] - padded[:-2, 2:] + padded[:-2, :-2]
    grad_x = 0.5 * (upper_row - lower_row)
    grad_y = 0.5 * (right_col - left_col)
    second_x = upper_row - 2.0 * center + lower_row
    second_y = right_col - 2.0 * center + left_col
    cross_term = 0.25 * diagonal
    flow_term = (second_x * grad_y * grad_y - 2.0 * grad_x * grad_y * cross_term + second_y * grad_x * grad_x) / (1.0 + grad_x * grad_x + grad_y * grad_y)
    return center + flow_rate * flow_term

def reference(phi, target, defocus_ids, kernels, psi, row_freqs, col_freqs):
    scale_norm = 1.0 / jnp.sqrt(jnp.float32(WIN * COLS))
    row_cos, row_sin = tables(row_freqs, WIN, WIN)
    col_cos, col_sin = tables(col_freqs, COLS, COLS)
    inner_cos = row_cos[:, MARGIN:MARGIN + ROWS]
    inner_sin = row_sin[:, MARGIN:MARGIN + ROWS]
    middle = (LEVELS - 1) / 2.0
    defocus_all = (defocus_ids.astype(jnp.float32) - middle) / middle
    mask_pad = jnp.pad(jnp.tanh(phi).astype(jnp.bfloat16), ((MARGIN, MARGIN), (0, 0)))
    target_f = target.astype(jnp.float32)

    def strip_terms(index):
        start = index * ROWS
        window = lax.dynamic_slice_in_dim(mask_pad, start, WIN, 0)
        goal = lax.dynamic_slice_in_dim(target_f, start, ROWS, 0)
        p_re = product_t(window, col_cos).astype(jnp.bfloat16)
        p_im = (-product_t(window, col_sin)).astype(jnp.bfloat16)
        s_re = scale_norm * (product(row_cos, p_re) + product(row_sin, p_im))
        s_im = scale_norm * (product(row_cos, p_im) - product(row_sin, p_re))

        def plane_terms(defocus):
            phase_turn = defocus * psi
            cos_turn = jnp.cos(phase_turn)
            sin_turn = jnp.sin(phase_turn)
            k_re = kernels[0] * cos_turn - kernels[1] * sin_turn
            k_im = kernels[0] * sin_turn + kernels[1] * cos_turn
            g_re = (k_re * s_re - k_im * s_im).astype(jnp.bfloat16)
            g_im = (k_re * s_im + k_im * s_re).astype(jnp.bfloat16)
            q_re = (batch('fr,kfc->krc', inner_cos, g_re) - batch('fr,kfc->krc', inner_sin, g_im)).astype(jnp.bfloat16)
            q_im = (batch('fr,kfc->krc', inner_cos, g_im) + batch('fr,kfc->krc', inner_sin, g_re)).astype(jnp.bfloat16)
            e_re = scale_norm * (batch('krc,cy->kry', q_re, col_cos) - batch('krc,cy->kry', q_im, col_sin))
            e_im = scale_norm * (batch('krc,cy->kry', q_re, col_sin) + batch('krc,cy->kry', q_im, col_cos))
            intensity = lax.optimization_barrier(jnp.mean(e_re * e_re + e_im * e_im, axis=0))
            resist = jax.nn.sigmoid(slope_resist * (intensity - level_resist))
            weight = 4.0 * slope_resist / KERN * (resist - goal) * resist * (1.0 - resist)
            v_re = (weight * e_re).astype(jnp.bfloat16)
            v_im = (weight * e_im).astype(jnp.bfloat16)
            u_re = (batch('kry,cy->krc', v_re, col_cos) + batch('kry,cy->krc', v_im, col_sin)).astype(jnp.bfloat16)
            u_im = (batch('kry,cy->krc', v_im, col_cos) - batch('kry,cy->krc', v_re, col_sin)).astype(jnp.bfloat16)
            w_re = scale_norm * (batch('fr,krc->kfc', inner_cos, u_re) + batch('fr,krc->kfc', inner_sin, u_im))
            w_im = scale_norm * (batch('fr,krc->kfc', inner_cos, u_im) - batch('fr,krc->kfc', inner_sin, u_re))
            y_re = lax.optimization_barrier(jnp.sum(k_re * w_re + k_im * w_im, axis=0))
            y_im = lax.optimization_barrier(jnp.sum(k_re * w_im - k_im * w_re, axis=0))
            return (y_re, y_im)
        plane_re, plane_im = lax.map(plane_terms, defocus_all)
        z_re, z_im = spectral_rows(row_cos, row_sin, lax.optimization_barrier(jnp.sum(plane_re, axis=0)), lax.optimization_barrier(jnp.sum(plane_im, axis=0)))
        return scale_norm * (product(z_re, col_cos) - product(z_im, col_sin))
    windows = lax.map(strip_terms, jnp.arange(STRIPS, dtype=jnp.int32))
    from_prev = jnp.pad(windows[:-1, MARGIN + ROWS:], ((1, 0), (0, 0), (0, 0)))
    from_next = jnp.pad(windows[1:, :MARGIN], ((0, 1), (0, 0), (0, 0)))
    folded = windows[:, MARGIN:MARGIN + ROWS]
    folded = folded.at[:, :MARGIN].add(from_prev).at[:, ROWS - MARGIN:].add(from_next)
    folded = folded.reshape(STRIPS * ROWS, COLS)
    mask_slope = 1.0 - jnp.tanh(phi) * jnp.tanh(phi)
    level_set = phi - step_size * mask_slope * folded
    for counter in range(SWEEPS):
        level_set = curvature_step(jnp.pad(level_set, 1))
    return level_set
```

```python
import functools

import jax
import jax.numpy as jnp
from jax import lax
from jax.experimental import pallas as pl
from jax.experimental.pallas import tpu as pltpu
from jax.sharding import PartitionSpec as P

MARGIN = 64
LEVELS = 31
SWEEPS = 2
HALO = 8
LANES = 128
OFFSETS = (-2, -1, 1, 2)
MESH = pl.DeviceIdType.MESH

slope_resist = 4.0
level_resist = 0.5
step_size = 1.0
flow_rate = 0.2

SIN_TERMS = (1.0, -1.0 / 6.0, 1.0 / 120.0, -1.0 / 5040.0, 1.0 / 362880.0)
COS_TERMS = (1.0, -0.5, 1.0 / 24.0, -1.0 / 720.0, 1.0 / 40320.0)


def series(terms, square):
    total = jnp.full_like(square, terms[-1])
    for term in terms[-2::-1]:
        total = total * square + term
    return total


def turn_pair(turns):
    quarter = jnp.floor(4.0 * turns + 0.5)
    angle = (turns - 0.25 * quarter) * (2.0 * jnp.pi)
    square = angle * angle
    cos_0 = series(COS_TERMS, square)
    sin_0 = angle * series(SIN_TERMS, square)
    kind = quarter.astype(jnp.int32) & 3
    odd = (kind & 1) == 1
    cos_1 = jnp.where(odd, sin_0, cos_0)
    sin_1 = jnp.where(odd, cos_0, sin_0)
    cos_out = jnp.where((kind == 1) | (kind == 2), -cos_1, cos_1)
    sin_out = jnp.where(kind >= 2, -sin_1, sin_1)
    return cos_out, sin_out


def whole_turns(steps, period):
    return (steps - period * jnp.floor(steps * (1.0 / period) + 0.5)) * (1.0 / period)


def dot(lhs, rhs):
    return jnp.dot(lhs, rhs, preferred_element_type=jnp.float32)


def dot_t(lhs, rhs):
    return lax.dot_general(
        lhs, rhs, (((1,), (1,)), ((), ())), preferred_element_type=jnp.float32
    )


def iota(shape, dim):
    return lax.broadcasted_iota(jnp.int32, shape, dim)


def kernel(
    strips,
    planes,
    freqs_ref,
    defocus_ref,
    phi_ref,
    target_ref,
    kernels_ref,
    psi_ref,
    out_ref,
    table,
    freq_col,
    window,
    halo,
    k_re,
    k_im,
    spec,
    q_ref,
    v_ref,
    row_out,
    row_in,
    y_send,
    y_recv,
    y_sum,
    y_side,
    z_ref,
    grad,
    mask_send,
    mask_recv,
    halo_send,
    halo_recv,
    rs_send,
    rs_recv,
    side_send,
    side_recv,
    ag_send,
    ag_recv,
):
    rows, cols = phi_ref.shape
    kern, fr, fc = kernels_ref.shape[1:]
    chunks, _, wide = y_send.shape
    stride = planes // chunks
    win = rows + 2 * MARGIN
    ext = rows + 2 * HALO
    both = 2 * fr
    norm = float((win * cols) ** -0.5)
    bf16 = jnp.bfloat16
    strip = lax.axis_index("strip")
    focus = lax.axis_index("focus")

    def inside(offset):
        place = strip + offset
        return jnp.logical_and(place >= 0, place < strips)

    def to_strip(src, dst, send, recv, offset):
        return pltpu.make_async_remote_copy(
            src_ref=src,
            dst_ref=dst,
            send_sem=send,
            recv_sem=recv,
            device_id={"strip": strip + offset},
            device_id_type=MESH,
        )

    def to_focus(src, dst, send, recv, peer):
        return pltpu.make_async_remote_copy(
            src_ref=src,
            dst_ref=dst,
            send_sem=send,
            recv_sem=recv,
            device_id={"focus": peer},
            device_id_type=MESH,
        )

    barrier = pltpu.get_barrier_semaphore()
    for offset in OFFSETS:

        @pl.when(inside(offset))
        def _(offset=offset):
            pl.semaphore_signal(
                barrier, inc=1, device_id={"strip": strip + offset}, device_id_type=MESH
            )

    for step in range(1, planes):
        pl.semaphore_signal(
            barrier,
            inc=1,
            device_id={"focus": lax.rem(focus + step, planes)},
            device_id_type=MESH,
        )

    window[MARGIN : MARGIN + rows, :] = jnp.tanh(phi_ref[...]).astype(bf16)

    beside = jnp.minimum(strip, 2) + jnp.minimum(strips - 1 - strip, 2)
    pl.semaphore_wait(barrier, planes - 1 + beside)

    def mask_copy(offset):
        if offset == 1:
            src, dst, slot = window.at[rows : rows + MARGIN], window.at[:MARGIN], 0
        else:
            src, dst, slot = window.at[MARGIN : 2 * MARGIN], window.at[MARGIN + rows :], 1
        return to_strip(src, dst, mask_send.at[slot], mask_recv.at[slot], offset)

    def halo_copy(offset):
        if offset == 1:
            src, slot = phi_ref.at[rows - HALO :], 0
        else:
            src, slot = phi_ref.at[:HALO], 1
        return to_strip(src, halo.at[slot], halo_send.at[slot], halo_recv.at[slot], offset)

    for copy in (mask_copy, halo_copy):
        for offset in (1, -1):

            @pl.when(inside(offset))
            def _(copy=copy, offset=offset):
                copy(offset).start()

    for block in range(fc // LANES):
        lane_freqs = freqs_ref[:, block * LANES : (block + 1) * LANES]
        freq_col[block * LANES : (block + 1) * LANES, :] = jnp.broadcast_to(
            lane_freqs, (LANES, LANES)
        ).T
    group = 32
    for chunk in range(chunks):

        @pl.loop(0, wide // group)
        def _(step, chunk=chunk):
            first = pl.multiple_of(step * group, group)
            freq = freq_col[pl.ds(chunk * wide + first, group), :]
            lane = iota((group, LANES), 1).astype(jnp.float32)
            cos_now, sin_now = turn_pair(whole_turns(freq * lane, float(cols)))
            cos_turn, sin_turn = turn_pair(whole_turns(freq * float(LANES), float(cols)))
            for part in range(cols // LANES):
                here = slice(part * LANES, (part + 1) * LANES)
                table[pl.ds(2 * chunk * wide + first, group), here] = cos_now.astype(bf16)
                table[pl.ds((2 * chunk + 1) * wide + first, group), here] = sin_now.astype(bf16)
                cos_now, sin_now = (
                    cos_now * cos_turn - sin_now * sin_turn,
                    sin_now * cos_turn + cos_now * sin_turn,
                )

    row_lane = freqs_ref[:, fc : fc + LANES]
    row_sub = jnp.broadcast_to(row_lane, (LANES, LANES)).T[:both, :1]
    row_lane = row_lane[:, :both]

    def row_cosine(freq, place, quarters):
        turns = whole_turns(freq * place.astype(jnp.float32), float(win))
        return turn_pair(turns + 0.25 * quarters.astype(jnp.float32))[0]

    shape = (both, win)
    row_all = row_cosine(
        jnp.broadcast_to(row_sub, shape), iota(shape, 1), -(iota(shape, 0) // fr)
    ).astype(bf16)
    shape = (both, 2 * rows)
    row_in[...] = row_cosine(
        jnp.broadcast_to(row_sub, shape),
        MARGIN + iota(shape, 1) % rows,
        iota(shape, 0) // fr - iota(shape, 1) // rows,
    ).astype(bf16)
    shape = (2 * rows, both)
    row_back = row_cosine(
        jnp.broadcast_to(row_lane, shape),
        MARGIN + iota(shape, 0) % rows,
        iota(shape, 1) // fr - iota(shape, 0) // rows,
    ).astype(bf16)

    middle = (LEVELS - 1) / 2.0
    defocus = (defocus_ref[0].astype(jnp.float32) - middle) * (1.0 / middle)
    cos_turn, sin_turn = turn_pair(psi_ref[...] * (defocus * (0.5 / jnp.pi)))
    for k in range(kern):
        best_re, best_im = kernels_ref[0, k], kernels_ref[1, k]
        full_re = best_re * cos_turn - best_im * sin_turn
        full_im = best_re * sin_turn + best_im * cos_turn
        for chunk in range(chunks):
            k_re[k, chunk] = full_re[:, chunk * wide : (chunk + 1) * wide]
            k_im[k, chunk] = full_im[:, chunk * wide : (chunk + 1) * wide]

    for offset, copy, spot in ((-1, 1, slice(0, MARGIN)), (1, -1, slice(MARGIN + rows, win))):

        @pl.when(inside(offset))
        def _(copy=copy):
            mask_copy(copy).wait_recv()

        @pl.when(jnp.logical_not(inside(offset)))
        def _(spot=spot):
            window[spot, :] = jnp.zeros((MARGIN, cols), bf16)

    @pl.loop(0, chunks)
    def _(chunk):
        here = pl.ds(pl.multiple_of(chunk * 2 * wide, 2 * wide), 2 * wide)
        spec[:, here] = dot_t(window[...], table[here, :]).astype(bf16)

    halves = dot(row_all, spec[...])
    for k in range(kern):
        tops, lows = [], []
        for chunk in range(chunks):
            at_cos = slice(2 * chunk * wide, (2 * chunk + 1) * wide)
            at_sin = slice((2 * chunk + 1) * wide, (2 * chunk + 2) * wide)
            s_re = norm * (halves[:fr, at_cos] - halves[fr:, at_sin])
            s_im = -norm * (halves[:fr, at_sin] + halves[fr:, at_cos])
            tops.append(k_re[k, chunk] * s_re - k_im[k, chunk] * s_im)
            lows.append(k_re[k, chunk] * s_im + k_im[k, chunk] * s_re)
        g_pair = jnp.concatenate(
            [jnp.concatenate(tops, axis=1), jnp.concatenate(lows, axis=1)], axis=0
        ).astype(bf16)
        q_pair = dot(row_back, g_pair)
        own = slice(k * rows, (k + 1) * rows)
        turned = slice((kern + k) * rows, (kern + k + 1) * rows)
        for chunk in range(chunks):
            at_cos = slice(2 * chunk * wide, (2 * chunk + 1) * wide)
            at_sin = slice((2 * chunk + 1) * wide, (2 * chunk + 2) * wide)
            q_re = q_pair[:rows, chunk * wide : (chunk + 1) * wide].astype(bf16)
            q_im = q_pair[rows:, chunk * wide : (chunk + 1) * wide].astype(bf16)
            q_ref[own, at_cos] = q_re
            q_ref[own, at_sin] = -q_im
            q_ref[turned, at_cos] = q_im
            q_ref[turned, at_sin] = q_re

    piece = 256

    @pl.loop(0, cols // piece)
    def _(step):
        here = pl.ds(pl.multiple_of(step * piece, piece), piece)
        field = dot(q_ref[...], table[:, here]).reshape(2 * kern, rows, piece)
        intensity = (norm * norm / kern) * jnp.sum(field * field, axis=0)
        resist = 1.0 / (1.0 + jnp.exp(-slope_resist * (intensity - level_resist)))
        weight = (
            (norm * 4.0 * slope_resist / kern)
            * (resist - target_ref[:, here].astype(jnp.float32))
            * resist
            * (1.0 - resist)
        )
        v_ref[:, here] = (field * weight[None]).reshape(2 * kern * rows, piece).astype(bf16)

    half = kern * rows

    def adjoint(chunk):
        here = pl.ds(pl.multiple_of(chunk * 2 * wide, 2 * wide), 2 * wide)
        u_all = dot_t(v_ref[...], table[here, :])
        u_re = (u_all[:half, :wide] + u_all[half:, wide:]).astype(bf16)
        u_im = (u_all[half:, :wide] - u_all[:half, wide:]).astype(bf16)
        stacked = jnp.concatenate(
            [
                jnp.concatenate(
                    [u_re[k * rows : (k + 1) * rows], u_im[k * rows : (k + 1) * rows]], axis=0
                )
                for k in range(kern)
            ],
            axis=1,
        )
        w_all = norm * dot(row_in[...], stacked)
        y_re = jnp.zeros((fr, wide), jnp.float32)
        y_im = jnp.zeros((fr, wide), jnp.float32)
        for k in range(kern):
            w_re = w_all[:fr, k * wide : (k + 1) * wide]
            w_im = w_all[fr:, k * wide : (k + 1) * wide]
            y_re += k_re[k, chunk] * w_re + k_im[k, chunk] * w_im
            y_im += k_re[k, chunk] * w_im - k_im[k, chunk] * w_re
        y_send[chunk] = jnp.concatenate([y_re, y_im], axis=0).astype(bf16)

    def to_owner(chunk):
        return to_focus(
            y_send.at[chunk],
            y_recv.at[focus],
            rs_send.at[chunk],
            rs_recv.at[focus],
            chunk * stride,
        )

    mine = focus // stride
    owner = lax.rem(focus, stride) == 0
    for step in list(range(1, chunks)) + [0]:
        chunk = lax.rem(mine + step, chunks)
        adjoint(chunk)
        if step:
            to_owner(chunk).start()
        elif stride > 1:

            @pl.when(jnp.logical_not(owner))
            def _(chunk=chunk):
                to_owner(chunk).start()

    shape = (2 * ext, both)
    for index, offset in enumerate((0,) + OFFSETS):
        place = iota(shape, 0) % ext - HALO - offset * rows + MARGIN
        values = row_cosine(
            jnp.broadcast_to(row_lane, shape),
            place,
            iota(shape, 1) // fr - iota(shape, 0) // ext,
        )
        covered = jnp.logical_and(place >= 0, place < win)
        row_out[index] = jnp.where(covered, values, 0.0).astype(bf16)

    def side_copy(offset):
        slot = OFFSETS.index(-offset)
        return to_strip(y_sum, y_side.at[slot], side_send.at[slot], side_recv.at[slot], offset)

    def gather_copy(step):
        peer = lax.rem(focus + step, planes)
        return to_focus(z_ref.at[mine], z_ref.at[mine], ag_send.at[step], ag_recv.at[mine], peer)

    def own_part():
        total = y_send[mine].astype(jnp.float32)
        for step in range(1, planes):
            source = lax.rem(focus + step, planes)
            to_focus(
                y_send.at[0], y_recv.at[source], rs_send.at[0], rs_recv.at[source], source
            ).wait_recv()
            total += y_recv[source].astype(jnp.float32)
        y_sum[...] = total.astype(bf16)
        for offset in OFFSETS:

            @pl.when(inside(offset))
            def _(offset=offset):
                side_copy(offset).start()

        rows_z = dot(row_out[0], y_sum[...])
        for index, offset in enumerate(OFFSETS):

            @pl.when(inside(offset))
            def _(offset=offset):
                side_copy(-offset).wait_recv()

            @pl.when(jnp.logical_not(inside(offset)))
            def _(index=index):
                y_side[index] = jnp.zeros((both, wide), bf16)

            rows_z += dot(row_out[index + 1], y_side[index])
        z_ref[mine] = jnp.concatenate([rows_z[:ext], -rows_z[ext:]], axis=1).astype(bf16)
        for step in range(1, planes):
            gather_copy(step).start()

    if stride > 1:
        pl.when(owner)(own_part)
    else:
        own_part()

    def part_grad(chunk):
        here = pl.ds(pl.multiple_of(chunk * 2 * wide, 2 * wide), 2 * wide)
        return dot(z_ref[chunk], table[here, :])

    for step in range(chunks):
        chunk = lax.rem(mine + step, chunks)
        if step:
            to_focus(
                z_ref.at[chunk], z_ref.at[chunk], ag_send.at[0], ag_recv.at[chunk], chunk * stride
            ).wait_recv()
            grad[...] += part_grad(chunk)
        else:
            if stride > 1:

                @pl.when(jnp.logical_not(owner))
                def _(chunk=chunk):
                    to_focus(
                        z_ref.at[chunk],
                        z_ref.at[chunk],
                        ag_send.at[0],
                        ag_recv.at[chunk],
                        chunk * stride,
                    ).wait_recv()

            grad[...] = part_grad(chunk)

    for index, offset in enumerate((-1, 1)):

        @pl.when(inside(offset))
        def _(offset=offset):
            halo_copy(-offset).wait_recv()

        @pl.when(jnp.logical_not(inside(offset)))
        def _(index=index):
            halo[index] = jnp.zeros((HALO, cols), jnp.float32)

    level = jnp.concatenate([halo[0], phi_ref[...], halo[1]], axis=0)
    slope = jnp.tanh(level)
    row_place = strip * rows + iota((ext, cols), 0) - HALO
    in_tile = jnp.logical_and(row_place >= 0, row_place < strips * rows)
    level = level - (step_size * norm) * (1.0 - slope * slope) * grad[...]
    level = jnp.where(in_tile, level, 0.0)
    column = iota((ext, cols), 1)
    for sweep in range(SWEEPS):
        right = jnp.where(column == cols - 1, 0.0, pltpu.roll(level, cols - 1, 1))
        left = jnp.where(column == 0, 0.0, pltpu.roll(level, 1, 1))
        across = right - left
        upper = pltpu.roll(level, ext - 1, 0)
        lower = pltpu.roll(level, 1, 0)
        diagonal = pltpu.roll(across, ext - 1, 0) - pltpu.roll(across, 1, 0)
        grad_x = 0.5 * (upper - lower)
        grad_y = 0.5 * across
        second_x = upper - 2.0 * level + lower
        second_y = right - 2.0 * level + left
        cross = 0.25 * diagonal
        flow = (
            second_x * grad_y * grad_y - 2.0 * grad_x * grad_y * cross + second_y * grad_x * grad_x
        ) / (1.0 + grad_x * grad_x + grad_y * grad_y)
        level = jnp.where(in_tile, level + flow_rate * flow, 0.0)
    out_ref[...] = level[HALO : HALO + rows]

    for copy in (mask_copy, halo_copy):
        for offset in (1, -1):

            @pl.when(inside(offset))
            def _(copy=copy, offset=offset):
                copy(offset).wait_send()

    for step in range(chunks):
        chunk = lax.rem(mine + step, chunks)
        if step:
            to_owner(chunk).wait_send()
        elif stride > 1:

            @pl.when(jnp.logical_not(owner))
            def _(chunk=chunk):
                to_owner(chunk).wait_send()

    def own_sent():
        for offset in OFFSETS:

            @pl.when(inside(offset))
            def _(offset=offset):
                side_copy(offset).wait_send()

        for step in range(1, planes):
            gather_copy(step).wait_send()

    if stride > 1:
        pl.when(owner)(own_sent)
    else:
        own_sent()


def on_device(strips, planes, phi, target, defocus_ids, kernels, psi, row_freqs, col_freqs):
    rows, cols = phi.shape
    _, kern, fr, fc = kernels.shape
    wide = max(LANES, fc // planes)
    chunks = fc // wide
    ext = rows + 2 * HALO
    win = rows + 2 * MARGIN
    filler = jnp.zeros((LANES - 2 * fr,), jnp.int32)
    freqs = jnp.concatenate([col_freqs, row_freqs, row_freqs, filler]).astype(jnp.float32)[None]
    vmem = pl.BlockSpec(memory_space=pltpu.VMEM)
    smem = pl.BlockSpec(memory_space=pltpu.SMEM)
    bf16, f32 = jnp.bfloat16, jnp.float32
    return pl.pallas_call(
        functools.partial(kernel, strips, planes),
        out_shape=jax.ShapeDtypeStruct((rows, cols), f32),
        in_specs=[vmem, smem, vmem, vmem, vmem, vmem],
        out_specs=vmem,
        scratch_shapes=[
            pltpu.VMEM((2 * fc, cols), bf16),
            pltpu.VMEM((fc, LANES), f32),
            pltpu.VMEM((win, cols), bf16),
            pltpu.VMEM((2, HALO, cols), f32),
            pltpu.VMEM((kern, chunks, fr, wide), f32),
            pltpu.VMEM((kern, chunks, fr, wide), f32),
            pltpu.VMEM((win, 2 * fc), bf16),
            pltpu.VMEM((2 * kern * rows, 2 * fc), bf16),
            pltpu.VMEM((2 * kern * rows, cols), bf16),
            pltpu.VMEM((1 + len(OFFSETS), 2 * ext, 2 * fr), bf16),
            pltpu.VMEM((2 * fr, 2 * rows), bf16),
            pltpu.VMEM((chunks, 2 * fr, wide), bf16),
            pltpu.VMEM((planes, 2 * fr, wide), bf16),
            pltpu.VMEM((2 * fr, wide), bf16),
            pltpu.VMEM((len(OFFSETS), 2 * fr, wide), bf16),
            pltpu.VMEM((chunks, ext, 2 * wide), bf16),
            pltpu.VMEM((ext, cols), f32),
            pltpu.SemaphoreType.DMA((2,)),
            pltpu.SemaphoreType.DMA((2,)),
            pltpu.SemaphoreType.DMA((2,)),
            pltpu.SemaphoreType.DMA((2,)),
            pltpu.SemaphoreType.DMA((chunks,)),
            pltpu.SemaphoreType.DMA((planes,)),
            pltpu.SemaphoreType.DMA((len(OFFSETS),)),
            pltpu.SemaphoreType.DMA((len(OFFSETS),)),
            pltpu.SemaphoreType.DMA((planes,)),
            pltpu.SemaphoreType.DMA((chunks,)),
        ],
        compiler_params=pltpu.CompilerParams(
            collective_id=0, has_side_effects=True, vmem_limit_bytes=48 * 2**20
        ),
        cost_estimate=pl.CostEstimate(
            flops=2 * cols * 2 * fc * (win + ext + 4 * kern * rows),
            bytes_accessed=4 * (3 * rows * cols + 2 * kern * fr * fc),
            transcendentals=0,
        ),
    )(freqs, defocus_ids, phi, target, kernels, psi)


def solution(mesh):
    return jax.shard_map(
        functools.partial(on_device, mesh.shape["strip"], mesh.shape["focus"]),
        mesh=mesh,
        in_specs=(
            P(("tile", "strip"), None),
            P(("tile", "strip"), None),
            P(("tile", "focus")),
            P(),
            P(),
            P(),
            P(),
        ),
        out_specs=P(("tile", "strip"), None),
        check_vma=False,
    )
```

```python
import functools

import jax
import jax.numpy as jnp
from jax import lax
from jax.experimental import pallas as pl
from jax.experimental.pallas import tpu as pltpu
from jax.sharding import PartitionSpec as P

MARGIN = 64
LEVELS = 31
SWEEPS = 2
HALO = 8
LANES = 128
OFFSETS = (-2, -1, 1, 2)
MESH = pl.DeviceIdType.MESH

slope_resist = 4.0
level_resist = 0.5
step_size = 1.0
flow_rate = 0.2

SIN_TERMS = (1.0, -1.0 / 6.0, 1.0 / 120.0, -1.0 / 5040.0, 1.0 / 362880.0)
COS_TERMS = (1.0, -0.5, 1.0 / 24.0, -1.0 / 720.0, 1.0 / 40320.0)


def series(terms, square):
    total = jnp.full_like(square, terms[-1])
    for term in terms[-2::-1]:
        total = total * square + term
    return total


def turn_pair(turns):
    quarter = jnp.floor(4.0 * turns + 0.5)
    angle = (turns - 0.25 * quarter) * (2.0 * jnp.pi)
    square = angle * angle
    cos_0 = series(COS_TERMS, square)
    sin_0 = angle * series(SIN_TERMS, square)
    kind = quarter.astype(jnp.int32) & 3
    odd = (kind & 1) == 1
    cos_1 = jnp.where(odd, sin_0, cos_0)
    sin_1 = jnp.where(odd, cos_0, sin_0)
    cos_out = jnp.where((kind == 1) | (kind == 2), -cos_1, cos_1)
    sin_out = jnp.where(kind >= 2, -sin_1, sin_1)
    return cos_out, sin_out


def whole_turns(steps, period):
    return (steps - period * jnp.floor(steps * (1.0 / period) + 0.5)) * (1.0 / period)


def dot(lhs, rhs):
    return jnp.dot(lhs, rhs, preferred_element_type=jnp.float32)


def iota(shape, dim):
    return lax.broadcasted_iota(jnp.int32, shape, dim)


def kernel(
    strips,
    planes,
    defocus_ref,
    phi_hbm,
    target_hbm,
    kernels_hbm,
    psi_hbm,
    row_freqs_hbm,
    col_freqs_hbm,
    out_ref,
    phi_ref,
    target_ref,
    kernels_ref,
    psi_ref,
    row_freqs_ref,
    col_freqs_ref,
    load_sem,
    table,
    table_t,
    freq_col,
    window,
    halo,
    k_re,
    k_im,
    spec,
    q_ref,
    v_ref,
    row_out,
    row_in,
    y_send,
    y_recv,
    y_sum,
    y_side,
    z_ref,
    grad,
    slope_ref,
    level_ref,
    mask_send,
    mask_recv,
    halo_send,
    halo_recv,
    rs_send,
    rs_recv,
    side_send,
    side_recv,
    ag_send,
    ag_recv,
):
    rows, cols = phi_ref.shape
    kern, fr, fc = kernels_ref.shape[1:]
    chunks, _, wide = y_send.shape
    stride = planes // chunks
    win = rows + 2 * MARGIN
    ext = rows + 2 * HALO
    both = 2 * fr
    norm = float((win * cols) ** -0.5)
    bf16 = jnp.bfloat16
    strip = lax.axis_index("strip")
    focus = lax.axis_index("focus")

    def inside(offset):
        place = strip + offset
        return jnp.logical_and(place >= 0, place < strips)

    def to_strip(src, dst, send, recv, offset):
        return pltpu.make_async_remote_copy(
            src_ref=src,
            dst_ref=dst,
            send_sem=send,
            recv_sem=recv,
            device_id={"strip": strip + offset},
            device_id_type=MESH,
        )

    def to_focus(src, dst, send, recv, peer):
        return pltpu.make_async_remote_copy(
            src_ref=src,
            dst_ref=dst,
            send_sem=send,
            recv_sem=recv,
            device_id={"focus": peer},
            device_id_type=MESH,
        )

    pairs = (
        (phi_hbm, phi_ref),
        (col_freqs_hbm, col_freqs_ref),
        (row_freqs_hbm, row_freqs_ref),
        (psi_hbm, psi_ref),
        (kernels_hbm, kernels_ref),
        (target_hbm, target_ref),
    )
    loads = [
        pltpu.make_async_copy(src, dst, load_sem.at[index])
        for index, (src, dst) in enumerate(pairs)
    ]
    for load in loads:
        load.start()
    phi_load, col_load, row_load, psi_load, kernels_load, target_load = loads

    barrier = pltpu.get_barrier_semaphore()
    for offset in OFFSETS:

        @pl.when(inside(offset))
        def _(offset=offset):
            pl.semaphore_signal(
                barrier, inc=1, device_id={"strip": strip + offset}, device_id_type=MESH
            )

    for step in range(1, planes):
        pl.semaphore_signal(
            barrier,
            inc=1,
            device_id={"focus": lax.rem(focus + step, planes)},
            device_id_type=MESH,
        )

    phi_load.wait()
    window[MARGIN : MARGIN + rows, :] = jnp.tanh(phi_ref[...]).astype(bf16)

    col_load.wait()
    col_lane = col_freqs_ref[...].astype(jnp.float32)
    for block in range(fc // LANES):
        freq_col[block * LANES : (block + 1) * LANES, :] = jnp.broadcast_to(
            col_lane[:, block * LANES : (block + 1) * LANES], (LANES, LANES)
        ).T
    group = 32

    def table_rows(chunk):
        @pl.loop(0, wide // group)
        def _(step):
            first = pl.multiple_of(step * group, group)
            freq = freq_col[pl.ds(chunk * wide + first, group), :]
            lane = iota((group, LANES), 1).astype(jnp.float32)
            cos_now, sin_now = turn_pair(whole_turns(freq * lane, float(cols)))
            cos_turn, sin_turn = turn_pair(whole_turns(freq * float(LANES), float(cols)))
            for part in range(cols // LANES):
                here = slice(part * LANES, (part + 1) * LANES)
                table[pl.ds(2 * chunk * wide + first, group), here] = cos_now.astype(bf16)
                table[pl.ds((2 * chunk + 1) * wide + first, group), here] = sin_now.astype(bf16)
                cos_now, sin_now = (
                    cos_now * cos_turn - sin_now * sin_turn,
                    sin_now * cos_turn + cos_now * sin_turn,
                )

    segment = 16 * group

    def table_columns(block):
        freq = jnp.broadcast_to(col_lane[:, block * LANES : (block + 1) * LANES], (group, LANES))
        cos_turn, sin_turn = turn_pair(whole_turns(freq * float(group), float(cols)))
        at_cos = 2 * (block * LANES // wide) * wide + block * LANES % wide

        @pl.loop(0, cols // segment)
        def _(step):
            first = pl.multiple_of(step * segment, segment)
            place = (first + iota((group, LANES), 0)).astype(jnp.float32)
            cos_now, sin_now = turn_pair(whole_turns(freq * place, float(cols)))
            for part in range(segment // group):
                here = pl.ds(first + part * group, group)
                table_t[here, at_cos : at_cos + LANES] = cos_now.astype(bf16)
                table_t[here, at_cos + wide : at_cos + wide + LANES] = sin_now.astype(bf16)
                cos_now, sin_now = (
                    cos_now * cos_turn - sin_now * sin_turn,
                    sin_now * cos_turn + cos_now * sin_turn,
                )

    for block in range(fc // LANES):
        table_columns(block)

    beside = jnp.minimum(strip, 2) + jnp.minimum(strips - 1 - strip, 2)
    pl.semaphore_wait(barrier, planes - 1 + beside)

    def mask_copy(offset):
        if offset == 1:
            src, dst, slot = window.at[rows : rows + MARGIN], window.at[:MARGIN], 0
        else:
            src, dst, slot = window.at[MARGIN : 2 * MARGIN], window.at[MARGIN + rows :], 1
        return to_strip(src, dst, mask_send.at[slot], mask_recv.at[slot], offset)

    def halo_copy(offset):
        if offset == 1:
            src, slot = phi_ref.at[rows - HALO :], 0
        else:
            src, slot = phi_ref.at[:HALO], 1
        return to_strip(src, halo.at[slot], halo_send.at[slot], halo_recv.at[slot], offset)

    for offset in (1, -1):

        @pl.when(inside(offset))
        def _(offset=offset):
            mask_copy(offset).start()

    for chunk in range(chunks):
        table_rows(chunk)

    row_load.wait()
    row_once = row_freqs_ref[...].astype(jnp.float32)
    row_lane = jnp.concatenate(
        [row_once, row_once, jnp.zeros((1, LANES - both), jnp.float32)], axis=1
    )
    row_sub = jnp.broadcast_to(row_lane, (LANES, LANES)).T[:both, :1]
    row_lane = row_lane[:, :both]

    def row_cosine(freq, place, quarters):
        turns = whole_turns(freq * place.astype(jnp.float32), float(win))
        return turn_pair(turns + 0.25 * quarters.astype(jnp.float32))[0]

    shape = (both, win)
    row_all = row_cosine(
        jnp.broadcast_to(row_sub, shape), iota(shape, 1), -(iota(shape, 0) // fr)
    ).astype(bf16)
    shape = (both, 2 * rows)
    row_in[...] = row_cosine(
        jnp.broadcast_to(row_sub, shape),
        MARGIN + iota(shape, 1) % rows,
        iota(shape, 0) // fr - iota(shape, 1) // rows,
    ).astype(bf16)
    shape = (2 * rows, both)
    row_back = row_cosine(
        jnp.broadcast_to(row_lane, shape),
        MARGIN + iota(shape, 0) % rows,
        iota(shape, 1) // fr - iota(shape, 0) // rows,
    ).astype(bf16)

    middle = (LEVELS - 1) / 2.0
    defocus = (defocus_ref[0].astype(jnp.float32) - middle) * (1.0 / middle)
    psi_load.wait()
    kernels_load.wait()
    cos_turn, sin_turn = turn_pair(psi_ref[...] * (defocus * (0.5 / jnp.pi)))
    for k in range(kern):
        best_re, best_im = kernels_ref[0, k], kernels_ref[1, k]
        full_re = best_re * cos_turn - best_im * sin_turn
        full_im = best_re * sin_turn + best_im * cos_turn
        for chunk in range(chunks):
            k_re[k, chunk] = full_re[:, chunk * wide : (chunk + 1) * wide]
            k_im[k, chunk] = full_im[:, chunk * wide : (chunk + 1) * wide]

    for offset, copy, spot in ((-1, 1, slice(0, MARGIN)), (1, -1, slice(MARGIN + rows, win))):

        @pl.when(inside(offset))
        def _(copy=copy):
            mask_copy(copy).wait_recv()

        @pl.when(jnp.logical_not(inside(offset)))
        def _(spot=spot):
            window[spot, :] = jnp.zeros((MARGIN, cols), bf16)

    @pl.loop(0, chunks)
    def _(chunk):
        here = pl.ds(pl.multiple_of(chunk * 2 * wide, 2 * wide), 2 * wide)
        spec[:, here] = dot(window[...], table_t[:, here]).astype(bf16)

    for offset in (1, -1):

        @pl.when(inside(offset))
        def _(offset=offset):
            halo_copy(offset).start()

    halves = dot(row_all, spec[...])
    for k in range(kern):
        tops, lows = [], []
        for chunk in range(chunks):
            at_cos = slice(2 * chunk * wide, (2 * chunk + 1) * wide)
            at_sin = slice((2 * chunk + 1) * wide, (2 * chunk + 2) * wide)
            s_re = norm * (halves[:fr, at_cos] - halves[fr:, at_sin])
            s_im = -norm * (halves[:fr, at_sin] + halves[fr:, at_cos])
            tops.append(k_re[k, chunk] * s_re - k_im[k, chunk] * s_im)
            lows.append(k_re[k, chunk] * s_im + k_im[k, chunk] * s_re)
        g_pair = jnp.concatenate(
            [jnp.concatenate(tops, axis=1), jnp.concatenate(lows, axis=1)], axis=0
        ).astype(bf16)
        q_pair = dot(row_back, g_pair)
        own = slice(k * rows, (k + 1) * rows)
        turned = slice((kern + k) * rows, (kern + k + 1) * rows)
        for chunk in range(chunks):
            at_cos = slice(2 * chunk * wide, (2 * chunk + 1) * wide)
            at_sin = slice((2 * chunk + 1) * wide, (2 * chunk + 2) * wide)
            q_re = q_pair[:rows, chunk * wide : (chunk + 1) * wide].astype(bf16)
            q_im = q_pair[rows:, chunk * wide : (chunk + 1) * wide].astype(bf16)
            q_ref[own, at_cos] = q_re
            q_ref[own, at_sin] = -q_im
            q_ref[turned, at_cos] = q_im
            q_ref[turned, at_sin] = q_re

    piece = 256
    target_load.wait()

    def fields(step):
        return dot(q_ref[...], table[:, step * piece : (step + 1) * piece])

    ahead = fields(0)
    for step in range(cols // piece):
        here = slice(step * piece, (step + 1) * piece)
        field = ahead.reshape(2 * kern, rows, piece)
        if (step + 1) * piece < cols:
            ahead = fields(step + 1)
        intensity = (norm * norm / kern) * jnp.sum(field * field, axis=0)
        resist = 1.0 / (1.0 + jnp.exp(-slope_resist * (intensity - level_resist)))
        weight = (
            (norm * 4.0 * slope_resist / kern)
            * (resist - target_ref[:, here].astype(jnp.float32))
            * resist
            * (1.0 - resist)
        )
        v_ref[:, here] = (field * weight[None]).reshape(2 * kern * rows, piece).astype(bf16)

    half = kern * rows

    def adjoint(chunk):
        here = pl.ds(pl.multiple_of(chunk * 2 * wide, 2 * wide), 2 * wide)
        u_all = dot(v_ref[...], table_t[:, here])
        u_re = (u_all[:half, :wide] + u_all[half:, wide:]).astype(bf16)
        u_im = (u_all[half:, :wide] - u_all[:half, wide:]).astype(bf16)
        stacked = jnp.concatenate(
            [
                jnp.concatenate(
                    [u_re[k * rows : (k + 1) * rows], u_im[k * rows : (k + 1) * rows]], axis=0
                )
                for k in range(kern)
            ],
            axis=1,
        )
        w_all = norm * dot(row_in[...], stacked)
        y_re = jnp.zeros((fr, wide), jnp.float32)
        y_im = jnp.zeros((fr, wide), jnp.float32)
        for k in range(kern):
            w_re = w_all[:fr, k * wide : (k + 1) * wide]
            w_im = w_all[fr:, k * wide : (k + 1) * wide]
            y_re += k_re[k, chunk] * w_re + k_im[k, chunk] * w_im
            y_im += k_re[k, chunk] * w_im - k_im[k, chunk] * w_re
        y_send[chunk] = jnp.concatenate([y_re, y_im], axis=0).astype(bf16)

    def to_owner(chunk):
        return to_focus(
            y_send.at[chunk],
            y_recv.at[focus],
            rs_send.at[chunk],
            rs_recv.at[focus],
            chunk * stride,
        )

    mine = focus // stride
    owner = lax.rem(focus, stride) == 0
    for step in list(range(1, chunks)) + [0]:
        chunk = lax.rem(mine + step, chunks)
        adjoint(chunk)
        if step:
            to_owner(chunk).start()
        elif stride > 1:

            @pl.when(jnp.logical_not(owner))
            def _(chunk=chunk):
                to_owner(chunk).start()

    shape = (2 * ext, both)
    for index, offset in enumerate((0,) + OFFSETS):
        place = iota(shape, 0) % ext - HALO - offset * rows + MARGIN
        values = row_cosine(
            jnp.broadcast_to(row_lane, shape),
            place,
            iota(shape, 1) // fr - iota(shape, 0) // ext,
        )
        covered = jnp.logical_and(place >= 0, place < win)
        row_out[index] = jnp.where(covered, values, 0.0).astype(bf16)

    for index, offset in enumerate((-1, 1)):

        @pl.when(inside(offset))
        def _(offset=offset):
            halo_copy(-offset).wait_recv()

        @pl.when(jnp.logical_not(inside(offset)))
        def _(index=index):
            halo[index] = jnp.zeros((HALO, cols), jnp.float32)

    row_place = strip * rows + iota((ext, LANES), 0) - HALO
    kept = jnp.where(
        jnp.logical_and(row_place >= 0, row_place < strips * rows), 1.0, 0.0
    ).astype(jnp.float32)
    for spot, values in (
        (slice(0, HALO), halo.at[0]),
        (slice(HALO, HALO + rows), phi_ref),
        (slice(HALO + rows, ext), halo.at[1]),
    ):
        level_ref[0, spot, :] = values[...]
        mask = jnp.tanh(values[...])
        slope_ref[spot, :] = (step_size * norm) * (1.0 - mask * mask) * kept[spot, :1]

    def side_copy(offset):
        slot = OFFSETS.index(-offset)
        return to_strip(y_sum, y_side.at[slot], side_send.at[slot], side_recv.at[slot], offset)

    def gather_copy(step):
        peer = lax.rem(focus + step, planes)
        return to_focus(z_ref.at[mine], z_ref.at[mine], ag_send.at[step], ag_recv.at[mine], peer)

    def own_part():
        total = y_send[mine].astype(jnp.float32)
        for step in range(1, planes):
            source = lax.rem(focus + step, planes)
            to_focus(
                y_send.at[0], y_recv.at[source], rs_send.at[0], rs_recv.at[source], source
            ).wait_recv()
            total += y_recv[source].astype(jnp.float32)
        y_sum[...] = total.astype(bf16)
        for offset in OFFSETS:

            @pl.when(inside(offset))
            def _(offset=offset):
                side_copy(offset).start()

        rows_z = dot(row_out[0], y_sum[...])
        for index, offset in enumerate(OFFSETS):

            @pl.when(inside(offset))
            def _(offset=offset):
                side_copy(-offset).wait_recv()

            @pl.when(jnp.logical_not(inside(offset)))
            def _(index=index):
                y_side[index] = jnp.zeros((both, wide), bf16)

            rows_z += dot(row_out[index + 1], y_side[index])
        z_ref[mine] = jnp.concatenate([rows_z[:ext], -rows_z[ext:]], axis=1).astype(bf16)
        for step in range(1, planes):
            gather_copy(step).start()

    if stride > 1:
        pl.when(owner)(own_part)
    else:
        own_part()

    def arrived(chunk):
        to_focus(
            z_ref.at[chunk], z_ref.at[chunk], ag_send.at[0], ag_recv.at[chunk], chunk * stride
        ).wait_recv()

    for step in range(chunks):
        chunk = lax.rem(mine + step, chunks)
        if step:
            arrived(chunk)
        elif stride > 1:

            @pl.when(jnp.logical_not(owner))
            def _(chunk=chunk):
                arrived(chunk)

        here = pl.ds(pl.multiple_of(chunk * 2 * wide, 2 * wide), 2 * wide)
        for start in range(0, cols, piece):
            there = slice(start, start + piece)
            part = dot(z_ref[chunk], table[here, there])
            if step:
                part += grad[:, there]
            if step < chunks - 1:
                grad[:, there] = part
            else:
                level_ref[0, :, there] = level_ref[0, :, there] - slope_ref[:, there] * part

    lane = iota((ext, LANES), 1)
    empty = jnp.zeros((ext, LANES), jnp.float32)
    blocks = cols // LANES
    for sweep in range(SWEEPS):

        def load(block, sweep=sweep):
            if not 0 <= block < blocks:
                return empty, empty, empty
            center = level_ref[sweep % 2, :, block * LANES : (block + 1) * LANES]
            return center, pltpu.roll(center, LANES - 1, 1), pltpu.roll(center, 1, 1)

        before, now, after = load(-1), load(0), load(1)
        for block in range(blocks):
            level = now[0]
            right = jnp.where(lane == LANES - 1, after[1], now[1])
            left = jnp.where(lane == 0, before[2], now[2])
            across = right - left
            upper = pltpu.roll(level, ext - 1, 0)
            lower = pltpu.roll(level, 1, 0)
            along = upper - lower
            diagonal = pltpu.roll(across, ext - 1, 0) - pltpu.roll(across, 1, 0)
            twice = 2.0 * level
            second_x = upper + lower - twice
            second_y = right + left - twice
            along_2 = along * along
            across_2 = across * across
            flow = second_x * across_2 - 0.5 * (along * across) * diagonal + second_y * along_2
            level = level + flow_rate * flow / (4.0 + along_2 + across_2)
            there = slice(block * LANES, (block + 1) * LANES)
            if sweep < SWEEPS - 1:
                level_ref[(sweep + 1) % 2, :, there] = level * kept
            else:
                out_ref[:, there] = level[HALO : HALO + rows]
            before, now, after = now, after, load(block + 2)

    for copy in (mask_copy, halo_copy):
        for offset in (1, -1):

            @pl.when(inside(offset))
            def _(copy=copy, offset=offset):
                copy(offset).wait_send()

    for step in range(chunks):
        chunk = lax.rem(mine + step, chunks)
        if step:
            to_owner(chunk).wait_send()
        elif stride > 1:

            @pl.when(jnp.logical_not(owner))
            def _(chunk=chunk):
                to_owner(chunk).wait_send()

    def own_sent():
        for offset in OFFSETS:

            @pl.when(inside(offset))
            def _(offset=offset):
                side_copy(offset).wait_send()

        for step in range(1, planes):
            gather_copy(step).wait_send()

    if stride > 1:
        pl.when(owner)(own_sent)
    else:
        own_sent()


def on_device(strips, planes, phi, target, defocus_ids, kernels, psi, row_freqs, col_freqs):
    rows, cols = phi.shape
    _, kern, fr, fc = kernels.shape
    wide = max(LANES, fc // planes)
    chunks = fc // wide
    ext = rows + 2 * HALO
    win = rows + 2 * MARGIN
    vmem = pl.BlockSpec(memory_space=pltpu.VMEM)
    anywhere = pl.BlockSpec(memory_space=pl.ANY)
    smem = pl.BlockSpec(memory_space=pltpu.SMEM)
    bf16, f32 = jnp.bfloat16, jnp.float32
    return pl.pallas_call(
        functools.partial(kernel, strips, planes),
        out_shape=jax.ShapeDtypeStruct((rows, cols), f32),
        in_specs=[smem] + [anywhere] * 6,
        out_specs=vmem,
        scratch_shapes=[
            pltpu.VMEM(phi.shape, phi.dtype),
            pltpu.VMEM(target.shape, target.dtype),
            pltpu.VMEM(kernels.shape, kernels.dtype),
            pltpu.VMEM(psi.shape, psi.dtype),
            pltpu.VMEM((1, fr), row_freqs.dtype),
            pltpu.VMEM((1, fc), col_freqs.dtype),
            pltpu.SemaphoreType.DMA((6,)),
            pltpu.VMEM((2 * fc, cols), bf16),
            pltpu.VMEM((cols, 2 * fc), bf16),
            pltpu.VMEM((fc, LANES), f32),
            pltpu.VMEM((win, cols), bf16),
            pltpu.VMEM((2, HALO, cols), f32),
            pltpu.VMEM((kern, chunks, fr, wide), f32),
            pltpu.VMEM((kern, chunks, fr, wide), f32),
            pltpu.VMEM((win, 2 * fc), bf16),
            pltpu.VMEM((2 * kern * rows, 2 * fc), bf16),
            pltpu.VMEM((2 * kern * rows, cols), bf16),
            pltpu.VMEM((1 + len(OFFSETS), 2 * ext, 2 * fr), bf16),
            pltpu.VMEM((2 * fr, 2 * rows), bf16),
            pltpu.VMEM((chunks, 2 * fr, wide), bf16),
            pltpu.VMEM((planes, 2 * fr, wide), bf16),
            pltpu.VMEM((2 * fr, wide), bf16),
            pltpu.VMEM((len(OFFSETS), 2 * fr, wide), bf16),
            pltpu.VMEM((chunks, ext, 2 * wide), bf16),
            pltpu.VMEM((ext, cols), f32),
            pltpu.VMEM((ext, cols), f32),
            pltpu.VMEM((2, ext, cols), f32),
            pltpu.SemaphoreType.DMA((2,)),
            pltpu.SemaphoreType.DMA((2,)),
            pltpu.SemaphoreType.DMA((2,)),
            pltpu.SemaphoreType.DMA((2,)),
            pltpu.SemaphoreType.DMA((chunks,)),
            pltpu.SemaphoreType.DMA((planes,)),
            pltpu.SemaphoreType.DMA((len(OFFSETS),)),
            pltpu.SemaphoreType.DMA((len(OFFSETS),)),
            pltpu.SemaphoreType.DMA((planes,)),
            pltpu.SemaphoreType.DMA((chunks,)),
        ],
        compiler_params=pltpu.CompilerParams(
            collective_id=0, has_side_effects=True, vmem_limit_bytes=56 * 2**20
        ),
        cost_estimate=pl.CostEstimate(
            flops=2 * cols * 2 * fc * (win + ext + 4 * kern * rows),
            bytes_accessed=4 * (3 * rows * cols + 2 * kern * fr * fc),
            transcendentals=0,
        ),
    )(defocus_ids, phi, target, kernels, psi, row_freqs[None], col_freqs[None])


def solution(mesh):
    return jax.shard_map(
        functools.partial(on_device, mesh.shape["strip"], mesh.shape["focus"]),
        mesh=mesh,
        in_specs=(
            P(("tile", "strip"), None),
            P(("tile", "strip"), None),
            P(("tile", "focus")),
            P(),
            P(),
            P(),
            P(),
        ),
        out_specs=P(("tile", "strip"), None),
        check_vma=False,
    )
```

```python
import functools

import jax
import jax.numpy as jnp
from jax import lax
from jax.experimental import pallas as pl
from jax.experimental.pallas import tpu as pltpu
from jax.sharding import PartitionSpec as P

MARGIN = 64
LEVELS = 31
SWEEPS = 2
HALO = 8
LANES = 128
OFFSETS = (-2, -1, 1, 2)
MESH = pl.DeviceIdType.MESH

slope_resist = 4.0
level_resist = 0.5
step_size = 1.0
flow_rate = 0.2

SIN_TERMS = (1.0, -1.0 / 6.0, 1.0 / 120.0, -1.0 / 5040.0, 1.0 / 362880.0)
COS_TERMS = (1.0, -0.5, 1.0 / 24.0, -1.0 / 720.0, 1.0 / 40320.0)


def series(terms, square):
    total = jnp.full_like(square, terms[-1])
    for term in terms[-2::-1]:
        total = total * square + term
    return total


def turn_pair(turns):
    quarter = jnp.floor(4.0 * turns + 0.5)
    angle = (turns - 0.25 * quarter) * (2.0 * jnp.pi)
    square = angle * angle
    cos_0 = series(COS_TERMS, square)
    sin_0 = angle * series(SIN_TERMS, square)
    kind = quarter.astype(jnp.int32) & 3
    odd = (kind & 1) == 1
    cos_1 = jnp.where(odd, sin_0, cos_0)
    sin_1 = jnp.where(odd, cos_0, sin_0)
    cos_out = jnp.where((kind == 1) | (kind == 2), -cos_1, cos_1)
    sin_out = jnp.where(kind >= 2, -sin_1, sin_1)
    return cos_out, sin_out


def whole_turns(steps, period):
    return (steps - period * jnp.floor(steps * (1.0 / period) + 0.5)) * (1.0 / period)


def dot(lhs, rhs):
    return jnp.dot(lhs, rhs, preferred_element_type=jnp.float32)


def iota(shape, dim):
    return lax.broadcasted_iota(jnp.int32, shape, dim)


def kernel(
    strips,
    planes,
    defocus_ref,
    phi_hbm,
    target_hbm,
    kernels_hbm,
    psi_hbm,
    row_freqs_hbm,
    col_freqs_hbm,
    base_hbm,
    flow_hbm,
    phi_ref,
    target_ref,
    kernels_ref,
    psi_ref,
    row_freqs_ref,
    col_freqs_ref,
    load_sem,
    table,
    table_t,
    freq_col,
    window,
    halo,
    k_re,
    k_im,
    spec,
    q_ref,
    v_ref,
    row_out,
    row_in,
    y_send,
    y_recv,
    y_sum,
    y_side,
    z_ref,
    grad,
    slope_ref,
    level_ref,
    flow_ref,
    store_sem,
    mask_send,
    mask_recv,
    halo_send,
    halo_recv,
    rs_send,
    rs_recv,
    side_send,
    side_recv,
    ag_send,
    ag_recv,
):
    rows, cols = phi_ref.shape
    kern, fr, fc = kernels_ref.shape[1:]
    chunks, _, wide = y_send.shape
    stride = planes // chunks
    win = rows + 2 * MARGIN
    ext = rows + 2 * HALO
    both = 2 * fr
    norm = float((win * cols) ** -0.5)
    bf16 = jnp.bfloat16
    strip = lax.axis_index("strip")
    focus = lax.axis_index("focus")

    def inside(offset):
        place = strip + offset
        return jnp.logical_and(place >= 0, place < strips)

    def to_strip(src, dst, send, recv, offset):
        return pltpu.make_async_remote_copy(
            src_ref=src,
            dst_ref=dst,
            send_sem=send,
            recv_sem=recv,
            device_id={"strip": strip + offset},
            device_id_type=MESH,
        )

    def to_focus(src, dst, send, recv, peer):
        return pltpu.make_async_remote_copy(
            src_ref=src,
            dst_ref=dst,
            send_sem=send,
            recv_sem=recv,
            device_id={"focus": peer},
            device_id_type=MESH,
        )

    pairs = (
        (col_freqs_hbm, col_freqs_ref),
        (phi_hbm, phi_ref),
        (row_freqs_hbm, row_freqs_ref),
        (psi_hbm, psi_ref),
        (kernels_hbm, kernels_ref),
        (target_hbm, target_ref),
    )
    loads = [
        pltpu.make_async_copy(src, dst, load_sem.at[index])
        for index, (src, dst) in enumerate(pairs)
    ]
    for load in loads:
        load.start()
    col_load, phi_load, row_load, psi_load, kernels_load, target_load = loads

    barrier = pltpu.get_barrier_semaphore()
    for offset in OFFSETS:

        @pl.when(inside(offset))
        def _(offset=offset):
            pl.semaphore_signal(
                barrier, inc=1, device_id={"strip": strip + offset}, device_id_type=MESH
            )

    for step in range(1, planes):
        pl.semaphore_signal(
            barrier,
            inc=1,
            device_id={"focus": lax.rem(focus + step, planes)},
            device_id_type=MESH,
        )


    col_load.wait()
    col_lane = col_freqs_ref[...].astype(jnp.float32)
    for block in range(fc // LANES):
        freq_col[block * LANES : (block + 1) * LANES, :] = jnp.broadcast_to(
            col_lane[:, block * LANES : (block + 1) * LANES], (LANES, LANES)
        ).T
    group = 32

    def table_rows(chunk):
        @pl.loop(0, wide // group)
        def _(step):
            first = pl.multiple_of(step * group, group)
            freq = freq_col[pl.ds(chunk * wide + first, group), :]
            lane = iota((group, LANES), 1).astype(jnp.float32)
            cos_now, sin_now = turn_pair(whole_turns(freq * lane, float(cols)))
            cos_turn, sin_turn = turn_pair(whole_turns(freq * float(LANES), float(cols)))
            for part in range(cols // LANES):
                here = slice(part * LANES, (part + 1) * LANES)
                table[pl.ds(2 * chunk * wide + first, group), here] = cos_now.astype(bf16)
                table[pl.ds((2 * chunk + 1) * wide + first, group), here] = sin_now.astype(bf16)
                cos_now, sin_now = (
                    cos_now * cos_turn - sin_now * sin_turn,
                    sin_now * cos_turn + cos_now * sin_turn,
                )

    segment = 16 * group

    def table_columns(block):
        freq = jnp.broadcast_to(col_lane[:, block * LANES : (block + 1) * LANES], (group, LANES))
        cos_turn, sin_turn = turn_pair(whole_turns(freq * float(group), float(cols)))
        at_cos = 2 * (block * LANES // wide) * wide + block * LANES % wide

        @pl.loop(0, cols // segment)
        def _(step):
            first = pl.multiple_of(step * segment, segment)
            place = (first + iota((group, LANES), 0)).astype(jnp.float32)
            cos_now, sin_now = turn_pair(whole_turns(freq * place, float(cols)))
            for part in range(segment // group):
                here = pl.ds(first + part * group, group)
                table_t[here, at_cos : at_cos + LANES] = cos_now.astype(bf16)
                table_t[here, at_cos + wide : at_cos + wide + LANES] = sin_now.astype(bf16)
                cos_now, sin_now = (
                    cos_now * cos_turn - sin_now * sin_turn,
                    sin_now * cos_turn + cos_now * sin_turn,
                )

    def spec_copy(offset, chunk):
        if offset == 1:
            src, dst, slot = slice(rows, rows + MARGIN), slice(0, MARGIN), 0
        else:
            src, dst, slot = slice(MARGIN, 2 * MARGIN), slice(MARGIN + rows, win), 1
        return to_strip(
            spec.at[chunk, src],
            spec.at[chunk, dst],
            mask_send.at[slot, chunk],
            mask_recv.at[slot, chunk],
            offset,
        )

    def halo_copy(offset):
        if offset == 1:
            src, slot = phi_ref.at[rows - HALO :], 0
        else:
            src, slot = phi_ref.at[:HALO], 1
        return to_strip(src, halo.at[slot], halo_send.at[slot], halo_recv.at[slot], offset)

    def send_spec(chunk):
        for offset in (1, -1):

            @pl.when(inside(offset))
            def _(offset=offset):
                spec_copy(offset, chunk).start()

    greet = min(1, chunks - 1)
    for chunk in range(chunks):
        for block in range(chunk * wide // LANES, (chunk + 1) * wide // LANES):
            table_columns(block)
        if chunk == 0:
            phi_load.wait()
            window[...] = jnp.tanh(phi_ref[...]).astype(bf16)
        spec[chunk, MARGIN : MARGIN + rows, :] = dot(
            window[...], table_t[:, 2 * chunk * wide : 2 * (chunk + 1) * wide]
        ).astype(bf16)
        if chunk == greet:
            beside = jnp.minimum(strip, 2) + jnp.minimum(strips - 1 - strip, 2)
            pl.semaphore_wait(barrier, planes - 1 + beside)
            for earlier in range(chunk):
                send_spec(earlier)
        if chunk >= greet:
            send_spec(chunk)
    for chunk in range(chunks):
        table_rows(chunk)

    row_load.wait()
    row_once = row_freqs_ref[...].astype(jnp.float32)
    row_lane = jnp.concatenate(
        [row_once, row_once, jnp.zeros((1, LANES - both), jnp.float32)], axis=1
    )
    row_sub = jnp.broadcast_to(row_lane, (LANES, LANES)).T[:both, :1]
    row_lane = row_lane[:, :both]

    def row_cosine(freq, place, quarters):
        turns = whole_turns(freq * place.astype(jnp.float32), float(win))
        return turn_pair(turns + 0.25 * quarters.astype(jnp.float32))[0]

    shape = (both, win)
    row_all = row_cosine(
        jnp.broadcast_to(row_sub, shape), iota(shape, 1), -(iota(shape, 0) // fr)
    ).astype(bf16)
    shape = (both, 2 * rows)
    row_in[...] = row_cosine(
        jnp.broadcast_to(row_sub, shape),
        MARGIN + iota(shape, 1) % rows,
        iota(shape, 0) // fr - iota(shape, 1) // rows,
    ).astype(bf16)
    shape = (2 * rows, both)
    row_back = row_cosine(
        jnp.broadcast_to(row_lane, shape),
        MARGIN + iota(shape, 0) % rows,
        iota(shape, 1) // fr - iota(shape, 0) // rows,
    ).astype(bf16)

    middle = (LEVELS - 1) / 2.0
    defocus = (defocus_ref[0].astype(jnp.float32) - middle) * (1.0 / middle)
    psi_load.wait()
    kernels_load.wait()
    cos_turn, sin_turn = turn_pair(psi_ref[...] * (defocus * (0.5 / jnp.pi)))
    for k in range(kern):
        best_re, best_im = kernels_ref[0, k], kernels_ref[1, k]
        full_re = best_re * cos_turn - best_im * sin_turn
        full_im = best_re * sin_turn + best_im * cos_turn
        for chunk in range(chunks):
            k_re[k, chunk] = full_re[:, chunk * wide : (chunk + 1) * wide]
            k_im[k, chunk] = full_im[:, chunk * wide : (chunk + 1) * wide]

    halves = []
    for chunk in range(chunks):
        for offset, spot in ((-1, slice(0, MARGIN)), (1, slice(MARGIN + rows, win))):

            @pl.when(inside(offset))
            def _(offset=offset, chunk=chunk):
                spec_copy(-offset, chunk).wait_recv()

            @pl.when(jnp.logical_not(inside(offset)))
            def _(spot=spot, chunk=chunk):
                spec[chunk, spot, :] = jnp.zeros((MARGIN, 2 * wide), bf16)

        halves.append(dot(row_all, spec[chunk]))

    for offset in (1, -1):

        @pl.when(inside(offset))
        def _(offset=offset):
            halo_copy(offset).start()

    for k in range(kern):
        tops, lows = [], []
        for chunk in range(chunks):
            rows_cos, rows_sin = halves[chunk][:fr], halves[chunk][fr:]
            s_re = norm * (rows_cos[:, :wide] - rows_sin[:, wide:])
            s_im = -norm * (rows_cos[:, wide:] + rows_sin[:, :wide])
            tops.append(k_re[k, chunk] * s_re - k_im[k, chunk] * s_im)
            lows.append(k_re[k, chunk] * s_im + k_im[k, chunk] * s_re)
        g_pair = jnp.concatenate(
            [jnp.concatenate(tops, axis=1), jnp.concatenate(lows, axis=1)], axis=0
        ).astype(bf16)
        q_pair = dot(row_back, g_pair)
        own = slice(k * rows, (k + 1) * rows)
        turned = slice((kern + k) * rows, (kern + k + 1) * rows)
        for chunk in range(chunks):
            at_cos = slice(2 * chunk * wide, (2 * chunk + 1) * wide)
            at_sin = slice((2 * chunk + 1) * wide, (2 * chunk + 2) * wide)
            q_re = q_pair[:rows, chunk * wide : (chunk + 1) * wide].astype(bf16)
            q_im = q_pair[rows:, chunk * wide : (chunk + 1) * wide].astype(bf16)
            q_ref[own, at_cos] = q_re
            q_ref[own, at_sin] = -q_im
            q_ref[turned, at_cos] = q_im
            q_ref[turned, at_sin] = q_re

    piece = 256
    target_load.wait()

    def fields(step):
        return dot(q_ref[...], table[:, step * piece : (step + 1) * piece])

    ahead = fields(0)
    for step in range(cols // piece):
        here = slice(step * piece, (step + 1) * piece)
        field = ahead.reshape(2 * kern, rows, piece)
        if (step + 1) * piece < cols:
            ahead = fields(step + 1)
        intensity = (norm * norm / kern) * jnp.sum(field * field, axis=0)
        resist = 1.0 / (1.0 + jnp.exp(-slope_resist * (intensity - level_resist)))
        weight = (
            (norm * 4.0 * slope_resist / kern)
            * (resist - target_ref[:, here].astype(jnp.float32))
            * resist
            * (1.0 - resist)
        )
        v_ref[:, here] = (field * weight[None]).reshape(2 * kern * rows, piece).astype(bf16)

    half = kern * rows

    def adjoint(chunk):
        here = pl.ds(pl.multiple_of(chunk * 2 * wide, 2 * wide), 2 * wide)
        u_all = dot(v_ref[...], table_t[:, here])
        u_re = (u_all[:half, :wide] + u_all[half:, wide:]).astype(bf16)
        u_im = (u_all[half:, :wide] - u_all[:half, wide:]).astype(bf16)
        stacked = jnp.concatenate(
            [
                jnp.concatenate(
                    [u_re[k * rows : (k + 1) * rows], u_im[k * rows : (k + 1) * rows]], axis=0
                )
                for k in range(kern)
            ],
            axis=1,
        )
        w_all = norm * dot(row_in[...], stacked)
        y_re = jnp.zeros((fr, wide), jnp.float32)
        y_im = jnp.zeros((fr, wide), jnp.float32)
        for k in range(kern):
            w_re = w_all[:fr, k * wide : (k + 1) * wide]
            w_im = w_all[fr:, k * wide : (k + 1) * wide]
            y_re += k_re[k, chunk] * w_re + k_im[k, chunk] * w_im
            y_im += k_re[k, chunk] * w_im - k_im[k, chunk] * w_re
        y_send[chunk] = jnp.concatenate([y_re, y_im], axis=0).astype(bf16)

    def to_owner(chunk):
        return to_focus(
            y_send.at[chunk],
            y_recv.at[focus],
            rs_send.at[chunk],
            rs_recv.at[focus],
            chunk * stride,
        )

    mine = focus // stride
    owner = lax.rem(focus, stride) == 0
    for step in list(range(1, chunks)) + [0]:
        chunk = lax.rem(mine + step, chunks)
        adjoint(chunk)
        if step:
            to_owner(chunk).start()
        elif stride > 1:

            @pl.when(jnp.logical_not(owner))
            def _(chunk=chunk):
                to_owner(chunk).start()

    shape = (2 * ext, both)
    for index, offset in enumerate((0,) + OFFSETS):
        place = iota(shape, 0) % ext - HALO - offset * rows + MARGIN
        values = row_cosine(
            jnp.broadcast_to(row_lane, shape),
            place,
            iota(shape, 1) // fr - iota(shape, 0) // ext,
        )
        covered = jnp.logical_and(place >= 0, place < win)
        row_out[index] = jnp.where(covered, values, 0.0).astype(bf16)

    for index, offset in enumerate((-1, 1)):

        @pl.when(inside(offset))
        def _(offset=offset):
            halo_copy(-offset).wait_recv()

        @pl.when(jnp.logical_not(inside(offset)))
        def _(index=index):
            halo[index] = jnp.zeros((HALO, cols), jnp.float32)

    row_place = strip * rows + iota((ext, LANES), 0) - HALO
    kept = jnp.where(
        jnp.logical_and(row_place >= 0, row_place < strips * rows), 1.0, 0.0
    ).astype(jnp.float32)
    for spot, values in (
        (slice(0, HALO), halo.at[0]),
        (slice(HALO, HALO + rows), phi_ref),
        (slice(HALO + rows, ext), halo.at[1]),
    ):
        level_ref[0, spot, :] = values[...]
        mask = jnp.tanh(values[...])
        slope_ref[spot, :] = (step_size * norm) * (1.0 - mask * mask) * kept[spot, :1]

    def side_copy(offset):
        slot = OFFSETS.index(-offset)
        return to_strip(y_sum, y_side.at[slot], side_send.at[slot], side_recv.at[slot], offset)

    def gather_copy(step):
        peer = lax.rem(focus + step, planes)
        return to_focus(z_ref.at[mine], z_ref.at[mine], ag_send.at[step], ag_recv.at[mine], peer)

    def own_part():
        total = y_send[mine].astype(jnp.float32)
        for step in range(1, planes):
            source = lax.rem(focus + step, planes)
            to_focus(
                y_send.at[0], y_recv.at[source], rs_send.at[0], rs_recv.at[source], source
            ).wait_recv()
            total += y_recv[source].astype(jnp.float32)
        y_sum[...] = total.astype(bf16)
        for offset in OFFSETS:

            @pl.when(inside(offset))
            def _(offset=offset):
                side_copy(offset).start()

        rows_z = dot(row_out[0], y_sum[...])
        for index, offset in enumerate(OFFSETS):

            @pl.when(inside(offset))
            def _(offset=offset):
                side_copy(-offset).wait_recv()

            @pl.when(jnp.logical_not(inside(offset)))
            def _(index=index):
                y_side[index] = jnp.zeros((both, wide), bf16)

            rows_z += dot(row_out[index + 1], y_side[index])
        z_ref[mine] = jnp.concatenate([rows_z[:ext], -rows_z[ext:]], axis=1).astype(bf16)
        for step in range(1, planes):
            gather_copy(step).start()

    if stride > 1:
        pl.when(owner)(own_part)
    else:
        own_part()

    def arrived(chunk):
        to_focus(
            z_ref.at[chunk], z_ref.at[chunk], ag_send.at[0], ag_recv.at[chunk], chunk * stride
        ).wait_recv()

    for step in range(chunks):
        chunk = lax.rem(mine + step, chunks)
        if step:
            arrived(chunk)
        elif stride > 1:

            @pl.when(jnp.logical_not(owner))
            def _(chunk=chunk):
                arrived(chunk)

        here = pl.ds(pl.multiple_of(chunk * 2 * wide, 2 * wide), 2 * wide)
        for start in range(0, cols, piece):
            there = slice(start, start + piece)
            part = dot(z_ref[chunk], table[here, there])
            if step:
                part += grad[:, there]
            if step < chunks - 1:
                grad[:, there] = part
            else:
                level_ref[0, :, there] = level_ref[0, :, there] - slope_ref[:, there] * part

    lane = iota((ext, LANES), 1)
    empty = jnp.zeros((ext, LANES), jnp.float32)
    blocks = cols // LANES
    span = max(1, blocks // 4)
    last = (SWEEPS - 1) % 2

    def store(part):
        here = slice(part * span * LANES, (part + 1) * span * LANES)
        return pltpu.make_async_copy(
            flow_ref.at[:, here], flow_hbm.at[:, here], store_sem.at[1 + part]
        )

    store_base = pltpu.make_async_copy(
        level_ref.at[last, HALO : HALO + rows], base_hbm, store_sem.at[0]
    )
    for sweep in range(SWEEPS):
        if sweep == SWEEPS - 1:
            store_base.start()

        def load(block, sweep=sweep):
            if not 0 <= block < blocks:
                return empty, empty, empty
            center = level_ref[sweep % 2, :, block * LANES : (block + 1) * LANES]
            return center, pltpu.roll(center, LANES - 1, 1), pltpu.roll(center, 1, 1)

        before, now, after = load(-1), load(0), load(1)
        for block in range(blocks):
            level = now[0]
            right = jnp.where(lane == LANES - 1, after[1], now[1])
            left = jnp.where(lane == 0, before[2], now[2])
            across = right - left
            upper = pltpu.roll(level, ext - 1, 0)
            lower = pltpu.roll(level, 1, 0)
            along = upper - lower
            diagonal = pltpu.roll(across, ext - 1, 0) - pltpu.roll(across, 1, 0)
            twice = 2.0 * level
            second_x = upper + lower - twice
            second_y = right + left - twice
            along_2 = along * along
            across_2 = across * across
            flow = second_x * across_2 - 0.5 * (along * across) * diagonal + second_y * along_2
            flow = flow_rate * flow / (4.0 + along_2 + across_2)
            there = slice(block * LANES, (block + 1) * LANES)
            if sweep < SWEEPS - 1:
                level_ref[(sweep + 1) % 2, :, there] = (level + flow) * kept
            else:
                flow_ref[:, there] = flow[HALO : HALO + rows]
                if (block + 1) % span == 0:
                    store(block // span).start()
            before, now, after = now, after, load(block + 2)

    store_base.wait()
    for part in range(blocks // span):
        store(part).wait()

    for offset in (1, -1):

        @pl.when(inside(offset))
        def _(offset=offset):
            halo_copy(offset).wait_send()
            for chunk in range(chunks):
                spec_copy(offset, chunk).wait_send()

    for step in range(chunks):
        chunk = lax.rem(mine + step, chunks)
        if step:
            to_owner(chunk).wait_send()
        elif stride > 1:

            @pl.when(jnp.logical_not(owner))
            def _(chunk=chunk):
                to_owner(chunk).wait_send()

    def own_sent():
        for offset in OFFSETS:

            @pl.when(inside(offset))
            def _(offset=offset):
                side_copy(offset).wait_send()

        for step in range(1, planes):
            gather_copy(step).wait_send()

    if stride > 1:
        pl.when(owner)(own_sent)
    else:
        own_sent()


def on_device(strips, planes, phi, target, defocus_ids, kernels, psi, row_freqs, col_freqs):
    rows, cols = phi.shape
    _, kern, fr, fc = kernels.shape
    wide = max(LANES, fc // planes)
    chunks = fc // wide
    ext = rows + 2 * HALO
    win = rows + 2 * MARGIN
    hbm = pl.BlockSpec(memory_space=pltpu.HBM)
    smem = pl.BlockSpec(memory_space=pltpu.SMEM)
    bf16, f32 = jnp.bfloat16, jnp.float32
    base, flow = pl.pallas_call(
        functools.partial(kernel, strips, planes),
        out_shape=[jax.ShapeDtypeStruct((rows, cols), f32)] * 2,
        in_specs=[smem] + [hbm] * 6,
        out_specs=[hbm, hbm],
        scratch_shapes=[
            pltpu.VMEM(phi.shape, phi.dtype),
            pltpu.VMEM(target.shape, target.dtype),
            pltpu.VMEM(kernels.shape, kernels.dtype),
            pltpu.VMEM(psi.shape, psi.dtype),
            pltpu.VMEM((1, fr), row_freqs.dtype),
            pltpu.VMEM((1, fc), col_freqs.dtype),
            pltpu.SemaphoreType.DMA((6,)),
            pltpu.VMEM((2 * fc, cols), bf16),
            pltpu.VMEM((cols, 2 * fc), bf16),
            pltpu.VMEM((fc, LANES), f32),
            pltpu.VMEM((rows, cols), bf16),
            pltpu.VMEM((2, HALO, cols), f32),
            pltpu.VMEM((kern, chunks, fr, wide), f32),
            pltpu.VMEM((kern, chunks, fr, wide), f32),
            pltpu.VMEM((chunks, win, 2 * wide), bf16),
            pltpu.VMEM((2 * kern * rows, 2 * fc), bf16),
            pltpu.VMEM((2 * kern * rows, cols), bf16),
            pltpu.VMEM((1 + len(OFFSETS), 2 * ext, 2 * fr), bf16),
            pltpu.VMEM((2 * fr, 2 * rows), bf16),
            pltpu.VMEM((chunks, 2 * fr, wide), bf16),
            pltpu.VMEM((planes, 2 * fr, wide), bf16),
            pltpu.VMEM((2 * fr, wide), bf16),
            pltpu.VMEM((len(OFFSETS), 2 * fr, wide), bf16),
            pltpu.VMEM((chunks, ext, 2 * wide), bf16),
            pltpu.VMEM((ext, cols), f32),
            pltpu.VMEM((ext, cols), f32),
            pltpu.VMEM((2, ext, cols), f32),
            pltpu.VMEM((rows, cols), f32),
            pltpu.SemaphoreType.DMA((1 + cols // LANES,)),
            pltpu.SemaphoreType.DMA((2, chunks)),
            pltpu.SemaphoreType.DMA((2, chunks)),
            pltpu.SemaphoreType.DMA((2,)),
            pltpu.SemaphoreType.DMA((2,)),
            pltpu.SemaphoreType.DMA((chunks,)),
            pltpu.SemaphoreType.DMA((planes,)),
            pltpu.SemaphoreType.DMA((len(OFFSETS),)),
            pltpu.SemaphoreType.DMA((len(OFFSETS),)),
            pltpu.SemaphoreType.DMA((planes,)),
            pltpu.SemaphoreType.DMA((chunks,)),
        ],
        compiler_params=pltpu.CompilerParams(
            collective_id=0, has_side_effects=True, vmem_limit_bytes=58 * 2**20
        ),
        cost_estimate=pl.CostEstimate(
            flops=2 * cols * 2 * fc * (win + ext + 4 * kern * rows),
            bytes_accessed=4 * (3 * rows * cols + 2 * kern * fr * fc),
            transcendentals=0,
        ),
    )(defocus_ids, phi, target, kernels, psi, row_freqs[None], col_freqs[None])
    return base + flow


def solution(mesh):
    return jax.shard_map(
        functools.partial(on_device, mesh.shape["strip"], mesh.shape["focus"]),
        mesh=mesh,
        in_specs=(
            P(("tile", "strip"), None),
            P(("tile", "strip"), None),
            P(("tile", "focus")),
            P(),
            P(),
            P(),
            P(),
        ),
        out_specs=P(("tile", "strip"), None),
        check_vma=False,
    )
```

```python
import functools

import jax
import jax.numpy as jnp
from jax import lax
from jax.experimental import pallas as pl
from jax.experimental.pallas import tpu as pltpu
from jax.sharding import PartitionSpec as P

MARGIN = 64
LEVELS = 31
SWEEPS = 2
HALO = 8
LANES = 128
OFFSETS = (-1, 1, -2, 2)
MESH = pl.DeviceIdType.MESH

slope_resist = 4.0
level_resist = 0.5
step_size = 1.0
flow_rate = 0.2

SIN_TERMS = (1.0, -1.0 / 6.0, 1.0 / 120.0, -1.0 / 5040.0, 1.0 / 362880.0)
COS_TERMS = (1.0, -0.5, 1.0 / 24.0, -1.0 / 720.0, 1.0 / 40320.0)


def series(terms, square):
    total = jnp.full_like(square, terms[-1])
    for term in terms[-2::-1]:
        total = total * square + term
    return total


def turn_pair(turns):
    quarter = jnp.floor(4.0 * turns + 0.5)
    angle = (turns - 0.25 * quarter) * (2.0 * jnp.pi)
    square = angle * angle
    cos_0 = series(COS_TERMS, square)
    sin_0 = angle * series(SIN_TERMS, square)
    kind = quarter.astype(jnp.int32) & 3
    odd = (kind & 1) == 1
    cos_1 = jnp.where(odd, sin_0, cos_0)
    sin_1 = jnp.where(odd, cos_0, sin_0)
    cos_out = jnp.where((kind == 1) | (kind == 2), -cos_1, cos_1)
    sin_out = jnp.where(kind >= 2, -sin_1, sin_1)
    return cos_out, sin_out


def whole_turns(steps, period):
    return (steps - period * jnp.floor(steps * (1.0 / period) + 0.5)) * (1.0 / period)


def dot(lhs, rhs):
    return jnp.dot(lhs, rhs, preferred_element_type=jnp.float32)


def partner(me, step, count):
    if count & (count - 1):
        return lax.rem(me + step, count)
    place, bit = 0, 1
    while bit < count:
        digit = lax.rem(me // bit, 2)
        place = place + bit * (1 - digit if step & bit else digit)
        bit *= 2
    return place


def iota(shape, dim):
    return lax.broadcasted_iota(jnp.int32, shape, dim)


def kernel(
    strips,
    planes,
    defocus_ref,
    phi_hbm,
    target_hbm,
    kernels_hbm,
    psi_hbm,
    row_freqs_hbm,
    col_freqs_hbm,
    out_hbm,
    phi_ref,
    target_ref,
    kernels_ref,
    psi_ref,
    row_freqs_ref,
    col_freqs_ref,
    load_sem,
    table,
    table_t,
    freq_col,
    window,
    halo,
    k_re,
    k_im,
    spec,
    q_ref,
    v_ref,
    row_out,
    row_in,
    y_send,
    y_recv,
    y_sum,
    y_side,
    z_ref,
    grad,
    slope_ref,
    level_ref,
    out_ref,
    store_sem,
    mask_send,
    mask_recv,
    halo_send,
    halo_recv,
    rs_send,
    rs_recv,
    side_send,
    side_recv,
    ag_send,
    ag_recv,
):
    rows, cols = phi_ref.shape
    kern, fr, fc = kernels_ref.shape[1:]
    chunks, _, wide = y_send.shape
    stride = planes // chunks
    win = rows + 2 * MARGIN
    ext = rows + 2 * HALO
    both = 2 * fr
    norm = float((win * cols) ** -0.5)
    bf16 = jnp.bfloat16
    strip = lax.axis_index("strip")
    focus = lax.axis_index("focus")

    def inside(offset):
        place = strip + offset
        return jnp.logical_and(place >= 0, place < strips)

    def to_strip(src, dst, send, recv, offset):
        return pltpu.make_async_remote_copy(
            src_ref=src,
            dst_ref=dst,
            send_sem=send,
            recv_sem=recv,
            device_id={"strip": strip + offset},
            device_id_type=MESH,
        )

    def to_focus(src, dst, send, recv, peer):
        return pltpu.make_async_remote_copy(
            src_ref=src,
            dst_ref=dst,
            send_sem=send,
            recv_sem=recv,
            device_id={"focus": peer},
            device_id_type=MESH,
        )

    pairs = (
        (col_freqs_hbm, col_freqs_ref),
        (phi_hbm, phi_ref),
        (row_freqs_hbm, row_freqs_ref),
        (psi_hbm, psi_ref),
        (kernels_hbm, kernels_ref),
        (target_hbm, target_ref),
    )
    loads = [
        pltpu.make_async_copy(src, dst, load_sem.at[index])
        for index, (src, dst) in enumerate(pairs)
    ]
    for load in loads:
        load.start()
    col_load, phi_load, row_load, psi_load, kernels_load, target_load = loads

    barrier = pltpu.get_barrier_semaphore()
    for offset in OFFSETS:

        @pl.when(inside(offset))
        def _(offset=offset):
            pl.semaphore_signal(
                barrier, inc=1, device_id={"strip": strip + offset}, device_id_type=MESH
            )

    for step in range(1, planes):
        pl.semaphore_signal(
            barrier,
            inc=1,
            device_id={"focus": lax.rem(focus + step, planes)},
            device_id_type=MESH,
        )


    col_load.wait()
    col_lane = col_freqs_ref[...].astype(jnp.float32)
    for block in range(fc // LANES):
        freq_col[block * LANES : (block + 1) * LANES, :] = jnp.broadcast_to(
            col_lane[:, block * LANES : (block + 1) * LANES], (LANES, LANES)
        ).T
    group = 32

    def table_rows(chunk):
        @pl.loop(0, wide // group)
        def _(step):
            first = pl.multiple_of(step * group, group)
            freq = freq_col[pl.ds(chunk * wide + first, group), :]
            lane = iota((group, LANES), 1).astype(jnp.float32)
            cos_now, sin_now = turn_pair(whole_turns(freq * lane, float(cols)))
            cos_turn, sin_turn = turn_pair(whole_turns(freq * float(LANES), float(cols)))
            for part in range(cols // LANES):
                here = slice(part * LANES, (part + 1) * LANES)
                table[pl.ds(2 * chunk * wide + first, group), here] = cos_now.astype(bf16)
                table[pl.ds((2 * chunk + 1) * wide + first, group), here] = sin_now.astype(bf16)
                cos_now, sin_now = (
                    cos_now * cos_turn - sin_now * sin_turn,
                    sin_now * cos_turn + cos_now * sin_turn,
                )

    segment = 16 * group

    def table_columns(block):
        freq = jnp.broadcast_to(col_lane[:, block * LANES : (block + 1) * LANES], (group, LANES))
        cos_turn, sin_turn = turn_pair(whole_turns(freq * float(group), float(cols)))
        at_cos = 2 * (block * LANES // wide) * wide + block * LANES % wide

        @pl.loop(0, cols // segment)
        def _(step):
            first = pl.multiple_of(step * segment, segment)
            place = (first + iota((group, LANES), 0)).astype(jnp.float32)
            cos_now, sin_now = turn_pair(whole_turns(freq * place, float(cols)))
            for part in range(segment // group):
                here = pl.ds(first + part * group, group)
                table_t[here, at_cos : at_cos + LANES] = cos_now.astype(bf16)
                table_t[here, at_cos + wide : at_cos + wide + LANES] = sin_now.astype(bf16)
                cos_now, sin_now = (
                    cos_now * cos_turn - sin_now * sin_turn,
                    sin_now * cos_turn + cos_now * sin_turn,
                )

    def spec_copy(offset, chunk):
        if offset == 1:
            src, dst, slot = slice(rows, rows + MARGIN), slice(0, MARGIN), 0
        else:
            src, dst, slot = slice(MARGIN, 2 * MARGIN), slice(MARGIN + rows, win), 1
        return to_strip(
            spec.at[chunk, src],
            spec.at[chunk, dst],
            mask_send.at[slot, chunk],
            mask_recv.at[slot, chunk],
            offset,
        )

    def halo_copy(offset):
        if offset == 1:
            src, slot = phi_ref.at[rows - HALO :], 0
        else:
            src, slot = phi_ref.at[:HALO], 1
        return to_strip(src, halo.at[slot], halo_send.at[slot], halo_recv.at[slot], offset)

    even = lax.rem(strip, 2) == 0

    def send_spec(chunk):
        for side, offset in ((even, 1), (even, -1), (jnp.logical_not(even), -1), (jnp.logical_not(even), 1)):

            @pl.when(jnp.logical_and(side, inside(offset)))
            def _(offset=offset):
                spec_copy(offset, chunk).start()

    greet = min(1, chunks - 1)
    for chunk in range(chunks):
        for block in range(chunk * wide // LANES, (chunk + 1) * wide // LANES):
            table_columns(block)
        if chunk == 0:
            phi_load.wait()
            window[...] = jnp.tanh(phi_ref[...]).astype(bf16)
        spec[chunk, MARGIN : MARGIN + rows, :] = dot(
            window[...], table_t[:, 2 * chunk * wide : 2 * (chunk + 1) * wide]
        ).astype(bf16)
        if chunk == greet:
            beside = jnp.minimum(strip, 2) + jnp.minimum(strips - 1 - strip, 2)
            pl.semaphore_wait(barrier, planes - 1 + beside)
            for earlier in range(chunk):
                send_spec(earlier)
        if chunk >= greet:
            send_spec(chunk)
    for chunk in range(chunks):
        table_rows(chunk)

    row_load.wait()
    row_once = row_freqs_ref[...].astype(jnp.float32)
    row_lane = jnp.concatenate(
        [row_once, row_once, jnp.zeros((1, LANES - both), jnp.float32)], axis=1
    )
    row_sub = jnp.broadcast_to(row_lane, (LANES, LANES)).T[:both, :1]
    row_lane = row_lane[:, :both]

    def row_cosine(freq, place, quarters):
        turns = whole_turns(freq * place.astype(jnp.float32), float(win))
        return turn_pair(turns + 0.25 * quarters.astype(jnp.float32))[0]

    shape = (both, win)
    row_all = row_cosine(
        jnp.broadcast_to(row_sub, shape), iota(shape, 1), -(iota(shape, 0) // fr)
    ).astype(bf16)
    shape = (both, 2 * rows)
    row_in[...] = row_cosine(
        jnp.broadcast_to(row_sub, shape),
        MARGIN + iota(shape, 1) % rows,
        iota(shape, 0) // fr - iota(shape, 1) // rows,
    ).astype(bf16)
    shape = (2 * rows, both)
    row_back = row_cosine(
        jnp.broadcast_to(row_lane, shape),
        MARGIN + iota(shape, 0) % rows,
        iota(shape, 1) // fr - iota(shape, 0) // rows,
    ).astype(bf16)

    middle = (LEVELS - 1) / 2.0
    defocus = (defocus_ref[0].astype(jnp.float32) - middle) * (1.0 / middle)
    psi_load.wait()
    kernels_load.wait()
    cos_turn, sin_turn = turn_pair(psi_ref[...] * (defocus * (0.5 / jnp.pi)))
    for k in range(kern):
        best_re, best_im = kernels_ref[0, k], kernels_ref[1, k]
        full_re = best_re * cos_turn - best_im * sin_turn
        full_im = best_re * sin_turn + best_im * cos_turn
        for chunk in range(chunks):
            k_re[k, chunk] = full_re[:, chunk * wide : (chunk + 1) * wide]
            k_im[k, chunk] = full_im[:, chunk * wide : (chunk + 1) * wide]

    halves = []
    for chunk in range(chunks):
        for offset, spot in ((-1, slice(0, MARGIN)), (1, slice(MARGIN + rows, win))):

            @pl.when(inside(offset))
            def _(offset=offset, chunk=chunk):
                spec_copy(-offset, chunk).wait_recv()

            @pl.when(jnp.logical_not(inside(offset)))
            def _(spot=spot, chunk=chunk):
                spec[chunk, spot, :] = jnp.zeros((MARGIN, 2 * wide), bf16)

        halves.append(dot(row_all, spec[chunk]))

    for offset in (1, -1):

        @pl.when(inside(offset))
        def _(offset=offset):
            halo_copy(offset).start()

    for k in range(kern):
        tops, lows = [], []
        for chunk in range(chunks):
            rows_cos, rows_sin = halves[chunk][:fr], halves[chunk][fr:]
            s_re = norm * (rows_cos[:, :wide] - rows_sin[:, wide:])
            s_im = -norm * (rows_cos[:, wide:] + rows_sin[:, :wide])
            tops.append(k_re[k, chunk] * s_re - k_im[k, chunk] * s_im)
            lows.append(k_re[k, chunk] * s_im + k_im[k, chunk] * s_re)
        g_pair = jnp.concatenate(
            [jnp.concatenate(tops, axis=1), jnp.concatenate(lows, axis=1)], axis=0
        ).astype(bf16)
        q_pair = dot(row_back, g_pair)
        own = slice(k * rows, (k + 1) * rows)
        turned = slice((kern + k) * rows, (kern + k + 1) * rows)
        for chunk in range(chunks):
            at_cos = slice(2 * chunk * wide, (2 * chunk + 1) * wide)
            at_sin = slice((2 * chunk + 1) * wide, (2 * chunk + 2) * wide)
            q_re = q_pair[:rows, chunk * wide : (chunk + 1) * wide].astype(bf16)
            q_im = q_pair[rows:, chunk * wide : (chunk + 1) * wide].astype(bf16)
            q_ref[own, at_cos] = q_re
            q_ref[own, at_sin] = -q_im
            q_ref[turned, at_cos] = q_im
            q_ref[turned, at_sin] = q_re

    piece = 256
    target_load.wait()

    def fields(step):
        return dot(q_ref[...], table[:, step * piece : (step + 1) * piece])

    ahead = fields(0)
    for step in range(cols // piece):
        here = slice(step * piece, (step + 1) * piece)
        field = ahead.reshape(2 * kern, rows, piece)
        if (step + 1) * piece < cols:
            ahead = fields(step + 1)
        intensity = (norm * norm / kern) * jnp.sum(field * field, axis=0)
        resist = 1.0 / (1.0 + jnp.exp(-slope_resist * (intensity - level_resist)))
        weight = (
            (norm * 4.0 * slope_resist / kern)
            * (resist - target_ref[:, here].astype(jnp.float32))
            * resist
            * (1.0 - resist)
        )
        v_ref[:, here] = (field * weight[None]).reshape(2 * kern * rows, piece).astype(bf16)

    half = kern * rows

    def adjoint(chunk):
        here = pl.ds(pl.multiple_of(chunk * 2 * wide, 2 * wide), 2 * wide)
        u_all = dot(v_ref[...], table_t[:, here])
        u_re = (u_all[:half, :wide] + u_all[half:, wide:]).astype(bf16)
        u_im = (u_all[half:, :wide] - u_all[:half, wide:]).astype(bf16)
        stacked = jnp.concatenate(
            [
                jnp.concatenate(
                    [u_re[k * rows : (k + 1) * rows], u_im[k * rows : (k + 1) * rows]], axis=0
                )
                for k in range(kern)
            ],
            axis=1,
        )
        w_all = norm * dot(row_in[...], stacked)
        y_re = jnp.zeros((fr, wide), jnp.float32)
        y_im = jnp.zeros((fr, wide), jnp.float32)
        for k in range(kern):
            w_re = w_all[:fr, k * wide : (k + 1) * wide]
            w_im = w_all[fr:, k * wide : (k + 1) * wide]
            y_re += k_re[k, chunk] * w_re + k_im[k, chunk] * w_im
            y_im += k_re[k, chunk] * w_im - k_im[k, chunk] * w_re
        y_send[chunk] = jnp.concatenate([y_re, y_im], axis=0).astype(bf16)

    def to_owner(chunk):
        return to_focus(
            y_send.at[chunk],
            y_recv.at[focus],
            rs_send.at[chunk],
            rs_recv.at[focus],
            chunk * stride,
        )

    mine = focus // stride
    owner = lax.rem(focus, stride) == 0
    for step in range(chunks - 1, -1, -1):
        chunk = partner(mine, step, chunks)
        adjoint(chunk)
        if step:
            to_owner(chunk).start()
        elif stride > 1:

            @pl.when(jnp.logical_not(owner))
            def _(chunk=chunk):
                to_owner(chunk).start()

    shape = (2 * ext, both)
    for index, offset in enumerate((0,) + OFFSETS):
        place = iota(shape, 0) % ext - HALO - offset * rows + MARGIN
        values = row_cosine(
            jnp.broadcast_to(row_lane, shape),
            place,
            iota(shape, 1) // fr - iota(shape, 0) // ext,
        )
        covered = jnp.logical_and(place >= 0, place < win)
        row_out[index] = jnp.where(covered, values, 0.0).astype(bf16)

    for index, offset in enumerate((-1, 1)):

        @pl.when(inside(offset))
        def _(offset=offset):
            halo_copy(-offset).wait_recv()

        @pl.when(jnp.logical_not(inside(offset)))
        def _(index=index):
            halo[index] = jnp.zeros((HALO, cols), jnp.float32)

    row_place = strip * rows + iota((ext, LANES), 0) - HALO
    kept = jnp.where(
        jnp.logical_and(row_place >= 0, row_place < strips * rows), 1.0, 0.0
    ).astype(jnp.float32)
    for spot, values in (
        (slice(0, HALO), halo.at[0]),
        (slice(HALO, HALO + rows), phi_ref),
        (slice(HALO + rows, ext), halo.at[1]),
    ):
        level_ref[0, spot, :] = values[...]
        mask = jnp.tanh(values[...])
        slope_ref[spot, :] = (step_size * norm) * (1.0 - mask * mask) * kept[spot, :1]

    def side_copy(offset):
        slot = OFFSETS.index(-offset)
        return to_strip(y_sum, y_side.at[slot], side_send.at[slot], side_recv.at[slot], offset)

    def gather_copy(step):
        peer = partner(focus, step, planes)
        return to_focus(z_ref.at[mine], z_ref.at[mine], ag_send.at[step], ag_recv.at[mine], peer)

    def own_part():
        total = y_send[mine].astype(jnp.float32)
        for step in range(1, planes):
            source = partner(focus, step, planes)
            to_focus(
                y_send.at[0], y_recv.at[source], rs_send.at[0], rs_recv.at[source], source
            ).wait_recv()
            total += y_recv[source].astype(jnp.float32)
        y_sum[...] = total.astype(bf16)
        for offset in OFFSETS:

            @pl.when(inside(offset))
            def _(offset=offset):
                side_copy(offset).start()

        rows_z = dot(row_out[0], y_sum[...])
        for index, offset in enumerate(OFFSETS):

            @pl.when(inside(offset))
            def _(offset=offset):
                side_copy(-offset).wait_recv()

            @pl.when(jnp.logical_not(inside(offset)))
            def _(index=index):
                y_side[index] = jnp.zeros((both, wide), bf16)

            rows_z += dot(row_out[index + 1], y_side[index])
        z_ref[mine] = jnp.concatenate([rows_z[:ext], -rows_z[ext:]], axis=1).astype(bf16)
        for step in range(planes - 1, 0, -1):
            gather_copy(step).start()

    if stride > 1:
        pl.when(owner)(own_part)
    else:
        own_part()

    def arrived(chunk):
        to_focus(
            z_ref.at[chunk], z_ref.at[chunk], ag_send.at[0], ag_recv.at[chunk], chunk * stride
        ).wait_recv()

    for step in range(chunks):
        chunk = partner(mine, step, chunks)
        if step:
            arrived(chunk)
        elif stride > 1:

            @pl.when(jnp.logical_not(owner))
            def _(chunk=chunk):
                arrived(chunk)

        here = pl.ds(pl.multiple_of(chunk * 2 * wide, 2 * wide), 2 * wide)
        for start in range(0, cols, piece):
            there = slice(start, start + piece)
            part = dot(z_ref[chunk], table[here, there])
            if step:
                part += grad[:, there]
            if step < chunks - 1:
                grad[:, there] = part
            else:
                level_ref[0, :, there] = level_ref[0, :, there] - slope_ref[:, there] * part

    lane = iota((ext, LANES), 1)
    empty = jnp.zeros((ext, LANES), jnp.float32)
    blocks = cols // LANES
    span = max(1, blocks // 4)

    def store(part):
        here = slice(part * span * LANES, (part + 1) * span * LANES)
        return pltpu.make_async_copy(
            out_ref.at[:, here], out_hbm.at[:, here], store_sem.at[part]
        )

    for sweep in range(SWEEPS):

        def load(block, sweep=sweep):
            if not 0 <= block < blocks:
                return empty, empty, empty
            center = level_ref[sweep % 2, :, block * LANES : (block + 1) * LANES]
            return center, pltpu.roll(center, LANES - 1, 1), pltpu.roll(center, 1, 1)

        before, now, after = load(-1), load(0), load(1)
        for block in range(blocks):
            level = now[0]
            right = jnp.where(lane == LANES - 1, after[1], now[1])
            left = jnp.where(lane == 0, before[2], now[2])
            across = right - left
            upper = pltpu.roll(level, ext - 1, 0)
            lower = pltpu.roll(level, 1, 0)
            along = upper - lower
            diagonal = pltpu.roll(across, ext - 1, 0) - pltpu.roll(across, 1, 0)
            twice = 2.0 * level
            second_x = upper + lower - twice
            second_y = right + left - twice
            along_2 = along * along
            across_2 = across * across
            flow = second_x * across_2 - 0.5 * (along * across) * diagonal + second_y * along_2
            flow = flow_rate * flow / (4.0 + along_2 + across_2)
            there = slice(block * LANES, (block + 1) * LANES)
            if sweep < SWEEPS - 1:
                level_ref[(sweep + 1) % 2, :, there] = (level + flow) * kept
            else:
                out_ref[:, there] = (level + flow)[HALO : HALO + rows]
                if (block + 1) % span == 0:
                    store(block // span).start()
            before, now, after = now, after, load(block + 2)

    for part in range(blocks // span):
        store(part).wait()

    for offset in (1, -1):

        @pl.when(inside(offset))
        def _(offset=offset):
            halo_copy(offset).wait_send()
            for chunk in range(chunks):
                spec_copy(offset, chunk).wait_send()

    for step in range(chunks):
        chunk = partner(mine, step, chunks)
        if step:
            to_owner(chunk).wait_send()
        elif stride > 1:

            @pl.when(jnp.logical_not(owner))
            def _(chunk=chunk):
                to_owner(chunk).wait_send()

    def own_sent():
        for offset in OFFSETS:

            @pl.when(inside(offset))
            def _(offset=offset):
                side_copy(offset).wait_send()

        for step in range(1, planes):
            gather_copy(step).wait_send()

    if stride > 1:
        pl.when(owner)(own_sent)
    else:
        own_sent()


def deliver(src_ref, dst_ref, sem):
    parts = sem.shape[0]
    depth = src_ref.shape[0] // parts
    copies = [
        pltpu.make_async_copy(
            src_ref.at[part * depth : (part + 1) * depth],
            dst_ref.at[part * depth : (part + 1) * depth],
            sem.at[part],
        )
        for part in range(parts)
    ]
    for copy in copies:
        copy.start()
    for copy in copies:
        copy.wait()


def on_device(strips, planes, phi, target, defocus_ids, kernels, psi, row_freqs, col_freqs):
    rows, cols = phi.shape
    _, kern, fr, fc = kernels.shape
    wide = max(LANES, fc // planes)
    chunks = fc // wide
    ext = rows + 2 * HALO
    win = rows + 2 * MARGIN
    hbm = pl.BlockSpec(memory_space=pltpu.HBM)
    smem = pl.BlockSpec(memory_space=pltpu.SMEM)
    bf16, f32 = jnp.bfloat16, jnp.float32
    level = pl.pallas_call(
        functools.partial(kernel, strips, planes),
        out_shape=jax.ShapeDtypeStruct((rows, cols), f32),
        in_specs=[smem] + [hbm] * 6,
        out_specs=hbm,
        scratch_shapes=[
            pltpu.VMEM(phi.shape, phi.dtype),
            pltpu.VMEM(target.shape, target.dtype),
            pltpu.VMEM(kernels.shape, kernels.dtype),
            pltpu.VMEM(psi.shape, psi.dtype),
            pltpu.VMEM((1, fr), row_freqs.dtype),
            pltpu.VMEM((1, fc), col_freqs.dtype),
            pltpu.SemaphoreType.DMA((6,)),
            pltpu.VMEM((2 * fc, cols), bf16),
            pltpu.VMEM((cols, 2 * fc), bf16),
            pltpu.VMEM((fc, LANES), f32),
            pltpu.VMEM((rows, cols), bf16),
            pltpu.VMEM((2, HALO, cols), f32),
            pltpu.VMEM((kern, chunks, fr, wide), f32),
            pltpu.VMEM((kern, chunks, fr, wide), f32),
            pltpu.VMEM((chunks, win, 2 * wide), bf16),
            pltpu.VMEM((2 * kern * rows, 2 * fc), bf16),
            pltpu.VMEM((2 * kern * rows, cols), bf16),
            pltpu.VMEM((1 + len(OFFSETS), 2 * ext, 2 * fr), bf16),
            pltpu.VMEM((2 * fr, 2 * rows), bf16),
            pltpu.VMEM((chunks, 2 * fr, wide), bf16),
            pltpu.VMEM((planes, 2 * fr, wide), bf16),
            pltpu.VMEM((2 * fr, wide), bf16),
            pltpu.VMEM((len(OFFSETS), 2 * fr, wide), bf16),
            pltpu.VMEM((chunks, ext, 2 * wide), bf16),
            pltpu.VMEM((ext, cols), f32),
            pltpu.VMEM((ext, cols), f32),
            pltpu.VMEM((2, ext, cols), f32),
            pltpu.VMEM((rows, cols), f32),
            pltpu.SemaphoreType.DMA((cols // LANES,)),
            pltpu.SemaphoreType.DMA((2, chunks)),
            pltpu.SemaphoreType.DMA((2, chunks)),
            pltpu.SemaphoreType.DMA((2,)),
            pltpu.SemaphoreType.DMA((2,)),
            pltpu.SemaphoreType.DMA((chunks,)),
            pltpu.SemaphoreType.DMA((planes,)),
            pltpu.SemaphoreType.DMA((len(OFFSETS),)),
            pltpu.SemaphoreType.DMA((len(OFFSETS),)),
            pltpu.SemaphoreType.DMA((planes,)),
            pltpu.SemaphoreType.DMA((chunks,)),
        ],
        compiler_params=pltpu.CompilerParams(
            collective_id=0, has_side_effects=True, vmem_limit_bytes=58 * 2**20
        ),
        cost_estimate=pl.CostEstimate(
            flops=2 * cols * 2 * fc * (win + ext + 4 * kern * rows),
            bytes_accessed=4 * (3 * rows * cols + 2 * kern * fr * fc),
            transcendentals=0,
        ),
    )(defocus_ids, phi, target, kernels, psi, row_freqs[None], col_freqs[None])
    return pl.pallas_call(
        deliver,
        out_shape=jax.ShapeDtypeStruct((rows, cols), f32),
        in_specs=[hbm],
        out_specs=hbm,
        scratch_shapes=[pltpu.SemaphoreType.DMA((rows // HALO,))],
        compiler_params=pltpu.CompilerParams(vmem_limit_bytes=58 * 2**20),
    )(level)


def solution(mesh):
    return jax.shard_map(
        functools.partial(on_device, mesh.shape["strip"], mesh.shape["focus"]),
        mesh=mesh,
        in_specs=(
            P(("tile", "strip"), None),
            P(("tile", "strip"), None),
            P(("tile", "focus")),
            P(),
            P(),
            P(),
            P(),
        ),
        out_specs=P(("tile", "strip"), None),
        check_vma=False,
    )
```

```python
import functools

import jax
import jax.numpy as jnp
from jax import lax
from jax.experimental import pallas as pl
from jax.experimental.pallas import tpu as pltpu
from jax.sharding import PartitionSpec as P

MARGIN = 64
LEVELS = 31
SWEEPS = 2
HALO = 8
LANES = 128
OFFSETS = (-1, 1, -2, 2)
MESH = pl.DeviceIdType.MESH

slope_resist = 4.0
level_resist = 0.5
step_size = 1.0
flow_rate = 0.2

SIN_TERMS = (1.0, -1.0 / 6.0, 1.0 / 120.0, -1.0 / 5040.0, 1.0 / 362880.0)
COS_TERMS = (1.0, -0.5, 1.0 / 24.0, -1.0 / 720.0, 1.0 / 40320.0)


def series(terms, square):
    total = jnp.full_like(square, terms[-1])
    for term in terms[-2::-1]:
        total = total * square + term
    return total


def turn_pair(turns):
    quarter = jnp.floor(4.0 * turns + 0.5)
    angle = (turns - 0.25 * quarter) * (2.0 * jnp.pi)
    square = angle * angle
    cos_0 = series(COS_TERMS, square)
    sin_0 = angle * series(SIN_TERMS, square)
    kind = quarter.astype(jnp.int32) & 3
    odd = (kind & 1) == 1
    cos_1 = jnp.where(odd, sin_0, cos_0)
    sin_1 = jnp.where(odd, cos_0, sin_0)
    cos_out = jnp.where((kind == 1) | (kind == 2), -cos_1, cos_1)
    sin_out = jnp.where(kind >= 2, -sin_1, sin_1)
    return cos_out, sin_out


def whole_turns(steps, period):
    return (steps - period * jnp.floor(steps * (1.0 / period) + 0.5)) * (1.0 / period)


def dot(lhs, rhs):
    return jnp.dot(lhs, rhs, preferred_element_type=jnp.float32)


def partner(me, step, count):
    if count & (count - 1):
        return lax.rem(me + step, count)
    place, bit = 0, 1
    while bit < count:
        digit = lax.rem(me // bit, 2)
        place = place + bit * (1 - digit if step & bit else digit)
        bit *= 2
    return place


def iota(shape, dim):
    return lax.broadcasted_iota(jnp.int32, shape, dim)


def kernel(
    strips,
    planes,
    defocus_ref,
    phi_hbm,
    target_hbm,
    kernels_hbm,
    psi_hbm,
    row_freqs_hbm,
    col_freqs_hbm,
    out_hbm,
    phi_ref,
    target_ref,
    kernels_ref,
    psi_ref,
    row_freqs_ref,
    col_freqs_ref,
    load_sem,
    table,
    table_t,
    freq_col,
    window,
    halo,
    k_re,
    k_im,
    spec,
    q_ref,
    v_ref,
    row_out,
    row_in,
    y_send,
    y_recv,
    y_sum,
    y_side,
    z_ref,
    grad,
    slope_ref,
    level_ref,
    out_ref,
    store_sem,
    mask_send,
    mask_recv,
    halo_send,
    halo_recv,
    rs_send,
    rs_recv,
    side_send,
    side_recv,
    ag_send,
    ag_recv,
):
    rows, cols = phi_ref.shape
    kern, fr, fc = kernels_ref.shape[1:]
    chunks, _, wide = y_send.shape
    stride = planes // chunks
    win = rows + 2 * MARGIN
    ext = rows + 2 * HALO
    both = 2 * fr
    norm = float((win * cols) ** -0.5)
    bf16 = jnp.bfloat16
    strip = lax.axis_index("strip")
    focus = lax.axis_index("focus")

    def inside(offset):
        place = strip + offset
        return jnp.logical_and(place >= 0, place < strips)

    def to_strip(src, dst, send, recv, offset):
        return pltpu.make_async_remote_copy(
            src_ref=src,
            dst_ref=dst,
            send_sem=send,
            recv_sem=recv,
            device_id={"strip": strip + offset},
            device_id_type=MESH,
        )

    def to_focus(src, dst, send, recv, peer):
        return pltpu.make_async_remote_copy(
            src_ref=src,
            dst_ref=dst,
            send_sem=send,
            recv_sem=recv,
            device_id={"focus": peer},
            device_id_type=MESH,
        )

    pairs = (
        (col_freqs_hbm, col_freqs_ref),
        (phi_hbm, phi_ref),
        (row_freqs_hbm, row_freqs_ref),
        (psi_hbm, psi_ref),
        (kernels_hbm, kernels_ref),
        (target_hbm, target_ref),
    )
    loads = [
        pltpu.make_async_copy(src, dst, load_sem.at[index])
        for index, (src, dst) in enumerate(pairs)
    ]
    for load in loads:
        load.start()
    col_load, phi_load, row_load, psi_load, kernels_load, target_load = loads

    barrier = pltpu.get_barrier_semaphore()
    for offset in OFFSETS:

        @pl.when(inside(offset))
        def _(offset=offset):
            pl.semaphore_signal(
                barrier, inc=1, device_id={"strip": strip + offset}, device_id_type=MESH
            )

    for step in range(1, planes):
        pl.semaphore_signal(
            barrier,
            inc=1,
            device_id={"focus": lax.rem(focus + step, planes)},
            device_id_type=MESH,
        )


    col_load.wait()
    col_lane = col_freqs_ref[...].astype(jnp.float32)
    turn_lane = turn_pair(whole_turns(col_lane * float(LANES), float(cols)))
    sign_lane = 1.0 - 2.0 * (col_lane - 2.0 * jnp.floor(0.5 * col_lane))
    for index, values in enumerate((col_lane, turn_lane[0], turn_lane[1], sign_lane)):
        for block in range(fc // LANES):
            here = slice(block * LANES, (block + 1) * LANES)
            freq_col[index, here, :] = jnp.broadcast_to(values[:, here], (LANES, LANES)).T
    group = 32
    middle_col = cols // 2

    def table_rows(chunk):
        @pl.loop(0, wide // group)
        def _(step):
            first = pl.multiple_of(step * group, group)
            spot = pl.ds(chunk * wide + first, group)
            freq = freq_col[0, spot, :]
            cos_turn, sin_turn = freq_col[1, spot, :], freq_col[2, spot, :]
            sign = freq_col[3, spot, :].astype(bf16)
            at_cos = pl.ds(2 * chunk * wide + first, group)
            at_sin = pl.ds((2 * chunk + 1) * wide + first, group)
            lane = iota((group, LANES), 1).astype(jnp.float32)
            cos_now, sin_now = turn_pair(whole_turns(freq * lane, float(cols)))
            for part in range(middle_col // LANES):
                here = slice(part * LANES, (part + 1) * LANES)
                beyond = slice(middle_col + part * LANES, middle_col + (part + 1) * LANES)
                cos_low, sin_low = cos_now.astype(bf16), sin_now.astype(bf16)
                table[at_cos, here] = cos_low
                table[at_sin, here] = sin_low
                table[at_cos, beyond] = cos_low * sign
                table[at_sin, beyond] = sin_low * sign
                cos_now, sin_now = (
                    cos_now * cos_turn - sin_now * sin_turn,
                    sin_now * cos_turn + cos_now * sin_turn,
                )

    segment = 16 * group

    def table_columns(block):
        freq = jnp.broadcast_to(col_lane[:, block * LANES : (block + 1) * LANES], (group, LANES))
        cos_turn, sin_turn = turn_pair(whole_turns(freq * float(group), float(cols)))
        sign = jnp.broadcast_to(
            sign_lane[:, block * LANES : (block + 1) * LANES], (group, LANES)
        ).astype(bf16)
        first_cos = 2 * (block * LANES // wide) * wide + block * LANES % wide
        at_cos = slice(first_cos, first_cos + LANES)
        at_sin = slice(first_cos + wide, first_cos + wide + LANES)

        @pl.loop(0, middle_col // segment)
        def _(step):
            first = pl.multiple_of(step * segment, segment)
            place = (first + iota((group, LANES), 0)).astype(jnp.float32)
            cos_now, sin_now = turn_pair(whole_turns(freq * place, float(cols)))
            for part in range(segment // group):
                here = pl.ds(first + part * group, group)
                beyond = pl.ds(middle_col + first + part * group, group)
                cos_low, sin_low = cos_now.astype(bf16), sin_now.astype(bf16)
                table_t[here, at_cos] = cos_low
                table_t[here, at_sin] = sin_low
                table_t[beyond, at_cos] = cos_low * sign
                table_t[beyond, at_sin] = sin_low * sign
                cos_now, sin_now = (
                    cos_now * cos_turn - sin_now * sin_turn,
                    sin_now * cos_turn + cos_now * sin_turn,
                )

    def spec_copy(offset, chunk):
        if offset == 1:
            src, dst, slot = slice(rows, rows + MARGIN), slice(0, MARGIN), 0
        else:
            src, dst, slot = slice(MARGIN, 2 * MARGIN), slice(MARGIN + rows, win), 1
        return to_strip(
            spec.at[chunk, src],
            spec.at[chunk, dst],
            mask_send.at[slot, chunk],
            mask_recv.at[slot, chunk],
            offset,
        )

    def halo_copy(offset):
        if offset == 1:
            src, slot = phi_ref.at[rows - HALO :], 0
        else:
            src, slot = phi_ref.at[:HALO], 1
        return to_strip(src, halo.at[slot], halo_send.at[slot], halo_recv.at[slot], offset)

    even = lax.rem(strip, 2) == 0

    def send_spec(chunk):
        for side, offset in ((even, 1), (even, -1), (jnp.logical_not(even), -1), (jnp.logical_not(even), 1)):

            @pl.when(jnp.logical_and(side, inside(offset)))
            def _(offset=offset):
                spec_copy(offset, chunk).start()

    greet = min(1, chunks - 1)
    for chunk in range(chunks):
        for block in range(chunk * wide // LANES, (chunk + 1) * wide // LANES):
            table_columns(block)
        if chunk == 0:
            phi_load.wait()
            window[...] = jnp.tanh(phi_ref[...]).astype(bf16)
        spec[chunk, MARGIN : MARGIN + rows, :] = dot(
            window[...], table_t[:, 2 * chunk * wide : 2 * (chunk + 1) * wide]
        ).astype(bf16)
        if chunk == greet:
            beside = jnp.minimum(strip, 2) + jnp.minimum(strips - 1 - strip, 2)
            pl.semaphore_wait(barrier, planes - 1 + beside)
            for earlier in range(chunk):
                send_spec(earlier)
        if chunk >= greet:
            send_spec(chunk)
    for chunk in range(chunks):
        table_rows(chunk)

    row_load.wait()
    row_once = row_freqs_ref[...].astype(jnp.float32)
    row_lane = jnp.concatenate(
        [row_once, row_once, jnp.zeros((1, LANES - both), jnp.float32)], axis=1
    )
    row_sub = jnp.broadcast_to(row_lane, (LANES, LANES)).T[:both, :1]
    row_lane = row_lane[:, :both]

    def row_cosine(freq, place, quarters):
        turns = whole_turns(freq * place.astype(jnp.float32), float(win))
        return turn_pair(turns + 0.25 * quarters.astype(jnp.float32))[0]

    shape = (both, win)
    row_all = row_cosine(
        jnp.broadcast_to(row_sub, shape), iota(shape, 1), -(iota(shape, 0) // fr)
    ).astype(bf16)
    shape = (both, 2 * rows)
    row_in[...] = row_cosine(
        jnp.broadcast_to(row_sub, shape),
        MARGIN + iota(shape, 1) % rows,
        iota(shape, 0) // fr - iota(shape, 1) // rows,
    ).astype(bf16)
    shape = (2 * rows, both)
    row_back = row_cosine(
        jnp.broadcast_to(row_lane, shape),
        MARGIN + iota(shape, 0) % rows,
        iota(shape, 1) // fr - iota(shape, 0) // rows,
    ).astype(bf16)

    middle = (LEVELS - 1) / 2.0
    defocus = (defocus_ref[0].astype(jnp.float32) - middle) * (1.0 / middle)
    psi_load.wait()
    kernels_load.wait()
    cos_turn, sin_turn = turn_pair(psi_ref[...] * (defocus * (0.5 / jnp.pi)))
    for k in range(kern):
        best_re, best_im = kernels_ref[0, k], kernels_ref[1, k]
        full_re = best_re * cos_turn - best_im * sin_turn
        full_im = best_re * sin_turn + best_im * cos_turn
        for chunk in range(chunks):
            k_re[k, chunk] = full_re[:, chunk * wide : (chunk + 1) * wide]
            k_im[k, chunk] = full_im[:, chunk * wide : (chunk + 1) * wide]

    halves = []
    for chunk in range(chunks):
        for offset, spot in ((-1, slice(0, MARGIN)), (1, slice(MARGIN + rows, win))):

            @pl.when(inside(offset))
            def _(offset=offset, chunk=chunk):
                spec_copy(-offset, chunk).wait_recv()

            @pl.when(jnp.logical_not(inside(offset)))
            def _(spot=spot, chunk=chunk):
                spec[chunk, spot, :] = jnp.zeros((MARGIN, 2 * wide), bf16)

        halves.append(dot(row_all, spec[chunk]))

    for offset in (1, -1):

        @pl.when(inside(offset))
        def _(offset=offset):
            halo_copy(offset).start()

    for k in range(kern):
        tops, lows = [], []
        for chunk in range(chunks):
            rows_cos, rows_sin = halves[chunk][:fr], halves[chunk][fr:]
            s_re = norm * (rows_cos[:, :wide] - rows_sin[:, wide:])
            s_im = -norm * (rows_cos[:, wide:] + rows_sin[:, :wide])
            tops.append(k_re[k, chunk] * s_re - k_im[k, chunk] * s_im)
            lows.append(k_re[k, chunk] * s_im + k_im[k, chunk] * s_re)
        g_pair = jnp.concatenate(
            [jnp.concatenate(tops, axis=1), jnp.concatenate(lows, axis=1)], axis=0
        ).astype(bf16)
        q_pair = dot(row_back, g_pair)
        own = slice(k * rows, (k + 1) * rows)
        turned = slice((kern + k) * rows, (kern + k + 1) * rows)
        for chunk in range(chunks):
            at_cos = slice(2 * chunk * wide, (2 * chunk + 1) * wide)
            at_sin = slice((2 * chunk + 1) * wide, (2 * chunk + 2) * wide)
            q_re = q_pair[:rows, chunk * wide : (chunk + 1) * wide].astype(bf16)
            q_im = q_pair[rows:, chunk * wide : (chunk + 1) * wide].astype(bf16)
            q_ref[own, at_cos] = q_re
            q_ref[own, at_sin] = -q_im
            q_ref[turned, at_cos] = q_im
            q_ref[turned, at_sin] = q_re

    piece = 256
    target_load.wait()

    def fields(step):
        return dot(q_ref[...], table[:, step * piece : (step + 1) * piece])

    ahead = fields(0)
    for step in range(cols // piece):
        here = slice(step * piece, (step + 1) * piece)
        field = ahead.reshape(2 * kern, rows, piece)
        if (step + 1) * piece < cols:
            ahead = fields(step + 1)
        intensity = (norm * norm / kern) * jnp.sum(field * field, axis=0)
        resist = 1.0 / (1.0 + jnp.exp(-slope_resist * (intensity - level_resist)))
        weight = (
            (norm * 4.0 * slope_resist / kern)
            * (resist - target_ref[:, here].astype(jnp.float32))
            * resist
            * (1.0 - resist)
        )
        v_ref[:, here] = (field * weight[None]).reshape(2 * kern * rows, piece).astype(bf16)

    half = kern * rows

    def adjoint(chunk):
        here = pl.ds(pl.multiple_of(chunk * 2 * wide, 2 * wide), 2 * wide)
        u_all = dot(v_ref[...], table_t[:, here])
        u_re = (u_all[:half, :wide] + u_all[half:, wide:]).astype(bf16)
        u_im = (u_all[half:, :wide] - u_all[:half, wide:]).astype(bf16)
        stacked = jnp.concatenate(
            [
                jnp.concatenate(
                    [u_re[k * rows : (k + 1) * rows], u_im[k * rows : (k + 1) * rows]], axis=0
                )
                for k in range(kern)
            ],
            axis=1,
        )
        w_all = norm * dot(row_in[...], stacked)
        y_re = jnp.zeros((fr, wide), jnp.float32)
        y_im = jnp.zeros((fr, wide), jnp.float32)
        for k in range(kern):
            w_re = w_all[:fr, k * wide : (k + 1) * wide]
            w_im = w_all[fr:, k * wide : (k + 1) * wide]
            y_re += k_re[k, chunk] * w_re + k_im[k, chunk] * w_im
            y_im += k_re[k, chunk] * w_im - k_im[k, chunk] * w_re
        y_send[chunk] = jnp.concatenate([y_re, y_im], axis=0).astype(bf16)

    def to_owner(chunk):
        return to_focus(
            y_send.at[chunk],
            y_recv.at[focus],
            rs_send.at[chunk],
            rs_recv.at[focus],
            chunk * stride,
        )

    mine = focus // stride
    owner = lax.rem(focus, stride) == 0
    for step in range(chunks - 1, -1, -1):
        chunk = partner(mine, step, chunks)
        adjoint(chunk)
        if step:
            to_owner(chunk).start()
        elif stride > 1:

            @pl.when(jnp.logical_not(owner))
            def _(chunk=chunk):
                to_owner(chunk).start()

    shape = (2 * ext, both)
    for index, offset in enumerate((0,) + OFFSETS):
        place = iota(shape, 0) % ext - HALO - offset * rows + MARGIN
        values = row_cosine(
            jnp.broadcast_to(row_lane, shape),
            place,
            iota(shape, 1) // fr - iota(shape, 0) // ext,
        )
        covered = jnp.logical_and(place >= 0, place < win)
        row_out[index] = jnp.where(covered, values, 0.0).astype(bf16)

    for index, offset in enumerate((-1, 1)):

        @pl.when(inside(offset))
        def _(offset=offset):
            halo_copy(-offset).wait_recv()

        @pl.when(jnp.logical_not(inside(offset)))
        def _(index=index):
            halo[index] = jnp.zeros((HALO, cols), jnp.float32)

    row_place = strip * rows + iota((ext, LANES), 0) - HALO
    kept = jnp.where(
        jnp.logical_and(row_place >= 0, row_place < strips * rows), 1.0, 0.0
    ).astype(jnp.float32)
    for spot, values in (
        (slice(0, HALO), halo.at[0]),
        (slice(HALO, HALO + rows), phi_ref),
        (slice(HALO + rows, ext), halo.at[1]),
    ):
        level_ref[0, spot, :] = values[...]
        mask = jnp.tanh(values[...])
        slope_ref[spot, :] = (step_size * norm) * (1.0 - mask * mask) * kept[spot, :1]

    def side_copy(offset):
        slot = OFFSETS.index(-offset)
        return to_strip(y_sum, y_side.at[slot], side_send.at[slot], side_recv.at[slot], offset)

    def gather_copy(step):
        peer = partner(focus, step, planes)
        return to_focus(z_ref.at[mine], z_ref.at[mine], ag_send.at[step], ag_recv.at[mine], peer)

    def own_part():
        total = y_send[mine].astype(jnp.float32)
        for step in range(1, planes):
            source = partner(focus, step, planes)
            to_focus(
                y_send.at[0], y_recv.at[source], rs_send.at[0], rs_recv.at[source], source
            ).wait_recv()
            total += y_recv[source].astype(jnp.float32)
        y_sum[...] = total.astype(bf16)
        for offset in OFFSETS:

            @pl.when(inside(offset))
            def _(offset=offset):
                side_copy(offset).start()

        rows_z = dot(row_out[0], y_sum[...])
        for index, offset in enumerate(OFFSETS):

            @pl.when(inside(offset))
            def _(offset=offset):
                side_copy(-offset).wait_recv()

            @pl.when(jnp.logical_not(inside(offset)))
            def _(index=index):
                y_side[index] = jnp.zeros((both, wide), bf16)

            rows_z += dot(row_out[index + 1], y_side[index])
        z_ref[mine] = jnp.concatenate([rows_z[:ext], -rows_z[ext:]], axis=1).astype(bf16)
        for step in range(planes - 1, 0, -1):
            gather_copy(step).start()

    if stride > 1:
        pl.when(owner)(own_part)
    else:
        own_part()

    def arrived(chunk):
        to_focus(
            z_ref.at[chunk], z_ref.at[chunk], ag_send.at[0], ag_recv.at[chunk], chunk * stride
        ).wait_recv()

    for step in range(chunks):
        chunk = partner(mine, step, chunks)
        if step:
            arrived(chunk)
        elif stride > 1:

            @pl.when(jnp.logical_not(owner))
            def _(chunk=chunk):
                arrived(chunk)

        here = pl.ds(pl.multiple_of(chunk * 2 * wide, 2 * wide), 2 * wide)
        for start in range(0, cols, piece):
            there = slice(start, start + piece)
            part = dot(z_ref[chunk], table[here, there])
            if step:
                part += grad[:, there]
            if step < chunks - 1:
                grad[:, there] = part
            else:
                level_ref[0, :, there] = level_ref[0, :, there] - slope_ref[:, there] * part

    lane = iota((ext, LANES), 1)
    empty = jnp.zeros((ext, LANES), jnp.float32)
    blocks = cols // LANES
    span = max(1, blocks // 4)

    def store(part):
        here = slice(part * span * LANES, (part + 1) * span * LANES)
        return pltpu.make_async_copy(
            out_ref.at[:, here], out_hbm.at[:, here], store_sem.at[part]
        )

    for sweep in range(SWEEPS):

        def load(block, sweep=sweep):
            if not 0 <= block < blocks:
                return empty, empty, empty
            center = level_ref[sweep % 2, :, block * LANES : (block + 1) * LANES]
            return center, pltpu.roll(center, LANES - 1, 1), pltpu.roll(center, 1, 1)

        before, now, after = load(-1), load(0), load(1)
        for block in range(blocks):
            level = now[0]
            right = jnp.where(lane == LANES - 1, after[1], now[1])
            left = jnp.where(lane == 0, before[2], now[2])
            across = right - left
            upper = pltpu.roll(level, ext - 1, 0)
            lower = pltpu.roll(level, 1, 0)
            along = upper - lower
            diagonal = pltpu.roll(across, ext - 1, 0) - pltpu.roll(across, 1, 0)
            twice = 2.0 * level
            second_x = upper + lower - twice
            second_y = right + left - twice
            along_2 = along * along
            across_2 = across * across
            flow = second_x * across_2 - 0.5 * (along * across) * diagonal + second_y * along_2
            flow = flow_rate * flow / (4.0 + along_2 + across_2)
            there = slice(block * LANES, (block + 1) * LANES)
            if sweep < SWEEPS - 1:
                level_ref[(sweep + 1) % 2, :, there] = (level + flow) * kept
            else:
                out_ref[:, there] = (level + flow)[HALO : HALO + rows]
                if (block + 1) % span == 0:
                    store(block // span).start()
            before, now, after = now, after, load(block + 2)

    for part in range(blocks // span):
        store(part).wait()

    for offset in (1, -1):

        @pl.when(inside(offset))
        def _(offset=offset):
            halo_copy(offset).wait_send()
            for chunk in range(chunks):
                spec_copy(offset, chunk).wait_send()

    for step in range(chunks):
        chunk = partner(mine, step, chunks)
        if step:
            to_owner(chunk).wait_send()
        elif stride > 1:

            @pl.when(jnp.logical_not(owner))
            def _(chunk=chunk):
                to_owner(chunk).wait_send()

    def own_sent():
        for offset in OFFSETS:

            @pl.when(inside(offset))
            def _(offset=offset):
                side_copy(offset).wait_send()

        for step in range(1, planes):
            gather_copy(step).wait_send()

    if stride > 1:
        pl.when(owner)(own_sent)
    else:
        own_sent()


def deliver(src_ref, dst_ref, held, load_sem, store_sem):
    parts = load_sem.shape[0]
    depth = src_ref.shape[0] // parts
    spots = [slice(part * depth, (part + 1) * depth) for part in range(parts)]
    loads = [
        pltpu.make_async_copy(src_ref.at[spot], held.at[spot], load_sem.at[part])
        for part, spot in enumerate(spots)
    ]
    stores = [
        pltpu.make_async_copy(held.at[spot], dst_ref.at[spot], store_sem.at[part])
        for part, spot in enumerate(spots)
    ]
    for load in loads:
        load.start()
    for load, store in zip(loads, stores):
        load.wait()
        store.start()
    for store in stores:
        store.wait()


def on_device(strips, planes, phi, target, defocus_ids, kernels, psi, row_freqs, col_freqs):
    rows, cols = phi.shape
    _, kern, fr, fc = kernels.shape
    wide = max(LANES, fc // planes)
    chunks = fc // wide
    ext = rows + 2 * HALO
    win = rows + 2 * MARGIN
    hbm = pl.BlockSpec(memory_space=pltpu.HBM)
    smem = pl.BlockSpec(memory_space=pltpu.SMEM)
    bf16, f32 = jnp.bfloat16, jnp.float32
    level = pl.pallas_call(
        functools.partial(kernel, strips, planes),
        out_shape=jax.ShapeDtypeStruct((rows, cols), f32),
        in_specs=[smem] + [hbm] * 6,
        out_specs=hbm,
        scratch_shapes=[
            pltpu.VMEM(phi.shape, phi.dtype),
            pltpu.VMEM(target.shape, target.dtype),
            pltpu.VMEM(kernels.shape, kernels.dtype),
            pltpu.VMEM(psi.shape, psi.dtype),
            pltpu.VMEM((1, fr), row_freqs.dtype),
            pltpu.VMEM((1, fc), col_freqs.dtype),
            pltpu.SemaphoreType.DMA((6,)),
            pltpu.VMEM((2 * fc, cols), bf16),
            pltpu.VMEM((cols, 2 * fc), bf16),
            pltpu.VMEM((4, fc, LANES), f32),
            pltpu.VMEM((rows, cols), bf16),
            pltpu.VMEM((2, HALO, cols), f32),
            pltpu.VMEM((kern, chunks, fr, wide), f32),
            pltpu.VMEM((kern, chunks, fr, wide), f32),
            pltpu.VMEM((chunks, win, 2 * wide), bf16),
            pltpu.VMEM((2 * kern * rows, 2 * fc), bf16),
            pltpu.VMEM((2 * kern * rows, cols), bf16),
            pltpu.VMEM((1 + len(OFFSETS), 2 * ext, 2 * fr), bf16),
            pltpu.VMEM((2 * fr, 2 * rows), bf16),
            pltpu.VMEM((chunks, 2 * fr, wide), bf16),
            pltpu.VMEM((planes, 2 * fr, wide), bf16),
            pltpu.VMEM((2 * fr, wide), bf16),
            pltpu.VMEM((len(OFFSETS), 2 * fr, wide), bf16),
            pltpu.VMEM((chunks, ext, 2 * wide), bf16),
            pltpu.VMEM((ext, cols), f32),
            pltpu.VMEM((ext, cols), f32),
            pltpu.VMEM((2, ext, cols), f32),
            pltpu.VMEM((rows, cols), f32),
            pltpu.SemaphoreType.DMA((cols // LANES,)),
            pltpu.SemaphoreType.DMA((2, chunks)),
            pltpu.SemaphoreType.DMA((2, chunks)),
            pltpu.SemaphoreType.DMA((2,)),
            pltpu.SemaphoreType.DMA((2,)),
            pltpu.SemaphoreType.DMA((chunks,)),
            pltpu.SemaphoreType.DMA((planes,)),
            pltpu.SemaphoreType.DMA((len(OFFSETS),)),
            pltpu.SemaphoreType.DMA((len(OFFSETS),)),
            pltpu.SemaphoreType.DMA((planes,)),
            pltpu.SemaphoreType.DMA((chunks,)),
        ],
        compiler_params=pltpu.CompilerParams(
            collective_id=0, has_side_effects=True, vmem_limit_bytes=58 * 2**20
        ),
        cost_estimate=pl.CostEstimate(
            flops=2 * cols * 2 * fc * (win + ext + 4 * kern * rows),
            bytes_accessed=4 * (3 * rows * cols + 2 * kern * fr * fc),
            transcendentals=0,
        ),
    )(defocus_ids, phi, target, kernels, psi, row_freqs[None], col_freqs[None])
    return pl.pallas_call(
        deliver,
        out_shape=jax.ShapeDtypeStruct((rows, cols), f32),
        in_specs=[hbm],
        out_specs=hbm,
        scratch_shapes=[
            pltpu.VMEM((rows, cols), f32),
            pltpu.SemaphoreType.DMA((4,)),
            pltpu.SemaphoreType.DMA((4,)),
        ],
        compiler_params=pltpu.CompilerParams(vmem_limit_bytes=58 * 2**20),
    )(level)


def solution(mesh):
    return jax.shard_map(
        functools.partial(on_device, mesh.shape["strip"], mesh.shape["focus"]),
        mesh=mesh,
        in_specs=(
            P(("tile", "strip"), None),
            P(("tile", "strip"), None),
            P(("tile", "focus")),
            P(),
            P(),
            P(),
            P(),
        ),
        out_specs=P(("tile", "strip"), None),
        check_vma=False,
    )
```
